512 devices in a mesh: seq: 64 (over y, z), head: 8 (over x, core).
Axes of the slice: x: 4, y: 8, z: 8, core: 2. Of those that a mesh axis runs over, the one named last changes fastest.
Arguments:
- tokens: bfloat16 [32768, 3072], P(('seq', 'head')), may hold values from -6 to 6
- qkv_weight: bfloat16 [3072, 3, 4096], P('seq', None, 'head'), may hold values from -0.109375 to 0.109375
- log_decay: float32 [32, 32768], P('head', 'seq'), may hold values from -1 to 0
- norm_gain: float32 [4096], P('head'), may hold values from 0.1 to 1.9
Outputs:
- attended: bfloat16 [32768, 4096], P(('seq', 'head'))
The draws below stay inside these ranges and needn't reach their ends.
All inputs are finite; a program needn't handle non-finite values.
Results may differ from the reference program's by a relative error of at most 0.0061.
Values may be sent and summed in bfloat16 or wider, within the bound.
No kernel may reach another device: no remote copies, remote signals or barrier semaphores. Data moves between devices by JAX's collectives and lax.ppermute only.
A program may use at most 64 MiB of HBM per device.

```python
import jax
import jax.numpy as jnp
from jax import lax

D = 3072
HEADS = 32
E = 128
BLK = 128
SEQUENCE_LENGTH = 32768


def draw_log_decay(key, part):
    key = jax.random.fold_in(key, 11)
    key_cat, key_slow, key_fast, key_mid, key_rough, key_where, key_drop = jax.random.split(key, 7)
    slow_rate = jnp.exp(jax.random.uniform(key_slow, (HEADS,), jnp.float32, jnp.log(0.2 / SEQUENCE_LENGTH), jnp.log(2.0 / SEQUENCE_LENGTH)))
    fast_rate = jnp.exp(jax.random.uniform(key_fast, (HEADS,), jnp.float32, jnp.log(1.0 / 50.0), jnp.log(1.0 / 30.0)))
    middle_rate = jnp.exp(jax.random.uniform(key_mid, (HEADS,), jnp.float32, jnp.log(2.0 / SEQUENCE_LENGTH), jnp.log(1.0 / 50.0)))
    category = jax.random.randint(key_cat, (HEADS,), 0, 4)
    forgetting_speed = jnp.where(category <= 1, slow_rate, jnp.where(category == 2, fast_rate, middle_rate))
    jagged_perturbation = jnp.exp(jax.random.uniform(key_rough, (HEADS, SEQUENCE_LENGTH), jnp.float32, jnp.log(0.5), jnp.log(2.0)))
    position_indices = jax.random.randint(key_where, (8,), 0, SEQUENCE_LENGTH)
    spike_occurrences = jnp.any(jnp.arange(SEQUENCE_LENGTH)[:, None] == position_indices[None, :], axis=1)
    forgetting_increments = jnp.log(jax.random.uniform(key_drop, (SEQUENCE_LENGTH,), jnp.float32, 0.5, 0.8))
    spike_indicator = jnp.where(spike_occurrences, forgetting_increments, 0.0)
    return -forgetting_speed[:, None] * jagged_perturbation + spike_indicator[None, :]


def block_levels(stream_key, extent, pieces, least, high):
    loudness = 1.0
    for axis_at, blocks in pieces:
        draws = jax.random.uniform(jax.random.fold_in(jax.random.fold_in(stream_key, 6), axis_at), (blocks,), jnp.float32, least / len(pieces), high / len(pieces))
        loudness = loudness * jnp.repeat(jnp.exp(draws), extent[axis_at] // blocks).reshape((-1,) + (1,) * (len(extent) - 1 - axis_at))
    return loudness


def gaussian(stream_key, shape, deviation, most, pieces=(), dtype=jnp.bfloat16):
    array = deviation * jax.random.normal(stream_key, shape, jnp.float32)
    if pieces:
        array = array * block_levels(stream_key, shape, pieces, -0.22, 0.18)
    return jnp.clip(array, -most, most).astype(dtype)


def setup_inputs(seed: int = 0) -> dict:
    arg_keys = jax.random.split(jax.random.key(seed), 5)
    tokens = gaussian(arg_keys[0], (SEQUENCE_LENGTH, D), 1.0, 6.0, ((0, 512),))
    qkv_weight = gaussian(arg_keys[1], (D, 3, HEADS * E), D ** -0.5, 0.109375, ((0, 64), (2, 8)))
    log_decay = draw_log_decay(jax.random.fold_in(arg_keys[4], 71), 0)
    norm_gain = jnp.clip(1.0 + 0.18 * jax.random.normal(arg_keys[3], (HEADS * E,), jnp.float32), 0.1, 1.9)
    return dict(tokens=tokens, qkv_weight=qkv_weight, log_decay=log_decay, norm_gain=norm_gain)


epsilon = 1e-05

def reference(tokens, qkv_weight, log_decay, norm_gain):
    block_count = SEQUENCE_LENGTH // BLK
    flat_weight = qkv_weight.reshape(D, 3 * HEADS * E)
    projected = jnp.dot(tokens, flat_weight, preferred_element_type=jnp.float32).astype(jnp.bfloat16)
    projected = projected.reshape(SEQUENCE_LENGTH, 3, HEADS, E).astype(jnp.float32)

    def blocked(field):
        return field.reshape(block_count, BLK, HEADS, E).transpose(0, 2, 1, 3)
    queries = blocked(projected[:, 0])
    key_rows = blocked(projected[:, 1])
    values = blocked(projected[:, 2])
    cumulative = jnp.cumsum(log_decay.reshape(HEADS, block_count, BLK).transpose(1, 0, 2), axis=2)
    causal_mask = jnp.arange(BLK)[:, None] >= jnp.arange(BLK)[None, :]
    high = lax.Precision.HIGHEST

    def advance(states, items):
        query_blk, key_blk, value_blk, decays = items
        gaps = decays[:, :, None] - decays[:, None, :]
        weights = jnp.exp(jnp.where(causal_mask[None], gaps, -1e+30))
        scores = jnp.einsum('hie,hje->hij', query_blk, key_blk, precision=high) * weights
        local_part = jnp.einsum('hij,hje->hie', scores, value_blk, precision=high)
        scaled_q = query_blk * jnp.exp(decays)[:, :, None]
        carried_part = jnp.einsum('hie,hef->hif', scaled_q, states, precision=high)
        last_decay = decays[:, -1]
        scaled_k = key_blk * jnp.exp(last_decay[:, None] - decays)[:, :, None]
        new_states = jnp.exp(last_decay)[:, None, None] * states + jnp.einsum('hje,hjf->hef', scaled_k, value_blk, precision=high)
        return (new_states, local_part + carried_part)
    initial = jnp.zeros((HEADS, E, E), jnp.float32)
    _, output = lax.scan(advance, initial, (queries, key_rows, values, cumulative))
    meansq = lax.optimization_barrier(jnp.mean(output * output, axis=3, keepdims=True))
    gained = output / jnp.sqrt(meansq + epsilon) * norm_gain.reshape(HEADS, E)[None, :, None, :]
    return gained.transpose(0, 2, 1, 3).reshape(SEQUENCE_LENGTH, HEADS * E).astype(jnp.bfloat16)
```

```python
import functools

import jax
import jax.numpy as jnp
from jax import lax
from jax.experimental import pallas as pl
from jax.experimental.pallas import tpu as pltpu
from jax.sharding import PartitionSpec as P

BLK = 128
E = 128
EPS = 1e-05
NY = 8
NZ = 8
NH = 8
EXTRA = 16
F32 = jnp.float32
BF16 = jnp.bfloat16
VMEM = pltpu.VMEM

Z_GROUPS = [[y * NZ + z for z in range(NZ)] for y in range(NY)]
OUT_GROUPS = [[g * 16 + i for i in range(16)] for g in range(NY * NZ // 2)]


def z_shift(d):
    return [(y * NZ + z, y * NZ + (z + d) % NZ) for y in range(NY) for z in range(NZ)]


def y_shift(d):
    return [(y * NZ + z, ((y + d) % NY) * NZ + z) for y in range(NY) for z in range(NZ)]


def y_later(d):
    return [(y * NZ + z, (y + d) * NZ + z) for y in range(NY - d) for z in range(NZ)]


PAIR = [(s, s ^ 1) for s in range(NY * NZ)]


def after(value, *earlier):
    return lax.optimization_barrier((value,) + earlier)[0]


def whole(count):
    return [pl.BlockSpec(memory_space=VMEM)] * count


def mm(a, b, dims=(((1,), (0,)), ((), ()))):
    return lax.dot_general(a, b, dims, preferred_element_type=F32)


def write_message(ref, head, state, decay):
    ref[head, :E, :] = state.astype(BF16)
    decay = jnp.broadcast_to(decay, (EXTRA, E))
    high = decay.astype(BF16)
    rest = decay - high.astype(F32)
    middle = rest.astype(BF16)
    low = (rest - middle.astype(F32)).astype(BF16)
    row = lax.broadcasted_iota(jnp.int32, (EXTRA, E), 0)
    part = jnp.where(row == 0, high.astype(F32), jnp.where(row == 1, middle.astype(F32), low.astype(F32)))
    ref[head, E:, :] = part.astype(BF16)


def read_decay(ref, head):
    rows = ref[head, E:, :].astype(F32)
    return (rows[0:1] + rows[1:2]) + rows[2:3]


def pieces_kernel(weight_ref, out_ref):
    for c in range(3):
        for i in range(NZ):
            half = slice((i % 2) * 256, (i % 2 + 1) * 256)
            out_ref[i, :, c * 256 : (c + 1) * 256] = weight_ref[c, :, half]


def order_kernel(sent_ref, out_ref):
    for s in range(2):
        for h in range(NH):
            out_ref[:, (h * 2 + s) * 256 : (h * 2 + s + 1) * 256] = sent_ref[s * NH + h]


def states_kernel(side_ref, own_ref, other_ref, col_ref, row_ref, proj_ref, prefix_ref, total_ref, message_ref):
    side = side_ref[0]
    proj_ref[side] = own_ref[...].astype(BF16)
    proj_ref[1 - side] = other_ref[...].astype(BF16)
    for head in range(2):
        state = jnp.zeros((E, E), F32)
        decay = jnp.zeros((1, 1), F32)
        for n in range(8):
            at = head * 8 + n
            rows = slice((n % 4) * BLK, (n % 4 + 1) * BLK)
            keys = proj_ref[n // 4, rows, 256 + head * E : 256 + (head + 1) * E]
            values = proj_ref[n // 4, rows, 512 + head * E : 512 + (head + 1) * E]
            last = row_ref[at : at + 1, BLK - 1 : BLK]
            scale = jnp.exp(last - col_ref[:, at : at + 1])
            prefix_ref[at] = state.astype(BF16)
            scaled = (keys.astype(F32) * scale).astype(BF16)
            state = jnp.exp(last) * state + mm(scaled, values, (((0,), (0,)), ((), ())))
            decay = decay + last
        total_ref[head] = state
        write_message(message_ref, head, state, decay)


def local_kernel(proj_ref, prefix_ref, col_ref, row_ref, out_ref):
    causal = lax.broadcasted_iota(jnp.int32, (BLK, BLK), 0) >= lax.broadcasted_iota(jnp.int32, (BLK, BLK), 1)
    for head in range(2):
        for n in range(8):
            at = head * 8 + n
            rows = slice((n % 4) * BLK, (n % 4 + 1) * BLK)
            queries = proj_ref[n // 4, rows, head * E : (head + 1) * E]
            keys = proj_ref[n // 4, rows, 256 + head * E : 256 + (head + 1) * E]
            values = proj_ref[n // 4, rows, 512 + head * E : 512 + (head + 1) * E]
            col = col_ref[:, at : at + 1]
            gaps = col - row_ref[at : at + 1, :]
            weights = jnp.exp(jnp.where(causal, gaps, -1e30))
            scores = mm(queries, keys, (((1,), (1,)), ((), ()))) * weights
            scaled = (queries.astype(F32) * jnp.exp(col)).astype(BF16)
            out_ref[at] = mm(scores.astype(BF16), values) + mm(scaled, prefix_ref[at])


def row_kernel(place_ref, total_ref, own_ref, m1_ref, m2_ref, m3_ref, before_ref, decay_ref, message_ref):
    place = place_ref[0]
    messages = (None, m1_ref, m2_ref, m3_ref)
    for head in range(2):
        mine = read_decay(own_ref, head)
        decays = [mine] + [read_decay(messages[k], head) for k in range(1, 4)]
        before = jnp.zeros((E, E), F32)
        later = jnp.zeros((E, E), F32)
        gone_before = jnp.zeros((1, E), F32)
        gone_later = jnp.zeros((1, E), F32)
        for k in range(1, 4):
            block = messages[k][head, :E, :].astype(F32)
            early = place >= k
            before = before + jnp.where(early, jnp.exp(gone_before), 0.0) * block
            later = later + jnp.where(early, 0.0, jnp.exp(gone_later)) * block
            gone_before = gone_before + jnp.where(early, decays[k], 0.0)
            gone_later = gone_later + jnp.where(early, 0.0, decays[k])
        through = jnp.exp(mine) * before + total_ref[head]
        before_ref[head] = before
        decay_ref[head] = jnp.broadcast_to(gone_before, (8, E))
        write_message(message_ref, head, later + jnp.exp(gone_later) * through, gone_before + mine + gone_later)


def final_kernel(*refs):
    messages = refs[:7]
    before_ref, decay_ref, part_ref, proj_ref, col_ref, start_ref, gain_ref, out_ref = refs[7:]
    for head in range(2):
        carried = jnp.zeros((E, E), F32)
        gone = jnp.zeros((1, E), F32)
        for ref in messages:
            carried = carried + jnp.exp(gone) * ref[head, :E, :].astype(F32)
            gone = gone + read_decay(ref, head)
        incoming = (jnp.exp(decay_ref[head, 0:1, :]) * carried + before_ref[head]).astype(BF16)
        gain = gain_ref[0:1, head * E : (head + 1) * E]
        for n in range(8):
            at = head * 8 + n
            rows = slice((n % 4) * BLK, (n % 4 + 1) * BLK)
            queries = proj_ref[n // 4, rows, head * E : (head + 1) * E]
            scale = jnp.exp(col_ref[:, at : at + 1] + start_ref[0:1, at : at + 1])
            scaled = (queries.astype(F32) * scale).astype(BF16)
            output = part_ref[at] + mm(scaled, incoming)
            meansq = jnp.mean(output * output, axis=1, keepdims=True)
            gained = output / jnp.sqrt(meansq + EPS) * gain
            out_ref[n * BLK : (n + 1) * BLK, head * E : (head + 1) * E] = gained.astype(BF16)


def call(kernel, outs, scalars, *args, flops=0):
    shapes = [jax.ShapeDtypeStruct(s, d) for s, d in outs]
    smem = [pl.BlockSpec(memory_space=pltpu.SMEM)] * len(scalars)
    moved = sum(a.size * a.dtype.itemsize for a in args)
    return pl.pallas_call(
        kernel,
        out_shape=shapes,
        in_specs=smem + whole(len(args)),
        out_specs=whole(len(outs)),
        cost_estimate=pl.CostEstimate(flops=flops, bytes_accessed=moved, transcendentals=0),
        compiler_params=pltpu.CompilerParams(vmem_limit_bytes=32 * 1024 * 1024),
    )(*scalars, *args)


def on_device(tokens, qkv_weight, log_decay, norm_gain):
    seq = lax.axis_index("seq")
    y, z = seq // NZ, seq % NZ
    side = z % 2
    place = z // 2
    side1 = side.reshape(1).astype(jnp.int32)
    place1 = place.reshape(1).astype(jnp.int32)

    pair_tokens = lax.ppermute(tokens, "seq", PAIR)
    own_rows = lax.all_gather(tokens, "head", axis=0, tiled=True)
    other_rows = lax.all_gather(pair_tokens, "head", axis=0, tiled=True)

    mine = lax.dynamic_slice_in_dim(log_decay, side * 2, 2, 0)
    theirs = lax.ppermute(lax.dynamic_slice_in_dim(log_decay, (1 - side) * 2, 2, 0), "seq", PAIR)
    both = jnp.where(side == 0, jnp.concatenate([mine, theirs], 1), jnp.concatenate([theirs, mine], 1))
    rows = jnp.cumsum(both.reshape(2, 8, BLK), axis=2)
    ends = rows[:, :, -1]
    starts = (jnp.cumsum(ends, axis=1) - ends).reshape(1, 16)
    rows = rows.reshape(16, BLK)
    cols = rows.T
    gain = lax.dynamic_slice_in_dim(norm_gain, side * 256, 256, 0).reshape(1, 256)

    (pieces,) = call(pieces_kernel, [((NZ, 48, 768), BF16)], [], qkv_weight.transpose(1, 0, 2))
    block = lax.all_to_all(pieces, "seq", split_axis=0, concat_axis=0, tiled=True, axis_index_groups=Z_GROUPS)
    block, rows, cols, starts, gain = lax.optimization_barrier((block, rows, cols, starts, gain))

    def add(total, tok, part, offset):
        x = lax.dynamic_slice_in_dim(tok, ((y + offset) % NY) * (NZ * 48), NZ * 48, 1)
        d = jnp.dot(x, part.reshape(NZ * 48, 768), preferred_element_type=F32)
        return d if total is None else total + d

    ups, downs = [block], [block]

    def hop(*earlier):
        up, down = lax.optimization_barrier((ups[-1], downs[-1]) + earlier)[:2]
        ups.append(lax.ppermute(up, "seq", y_shift(1)))
        downs.append(lax.ppermute(down, "seq", y_shift(-1)))

    def add_step(total, tok, step):
        if step == 0:
            return add(total, tok, block, 0)
        return add(add(total, tok, ups[step], -step), tok, downs[step], step)

    hop()
    own = add_step(None, own_rows, 0)
    hop(own)
    own = add_step(own, own_rows, 1)
    hop(own)
    own = add_step(own, own_rows, 2)
    other = add_step(add_step(None, other_rows, 0), other_rows, 1)
    up, down = lax.optimization_barrier((ups[3], downs[3], own, other))[:2]
    up4 = lax.ppermute(up[:4], "seq", y_shift(1))
    down4 = lax.ppermute(down[4:], "seq", y_shift(-1))
    own = add_step(own, own_rows, 3)
    other = add_step(add_step(other, other_rows, 2), other_rows, 3)
    up4, down4, own, other = lax.optimization_barrier((up4, down4, own, other))
    last = jnp.concatenate([up4, down4], 0)
    own = add(own, own_rows, last, 4)
    other = add(other, other_rows, last, 4)

    proj, prefix, total, message = call(
        states_kernel,
        [((2, 512, 768), BF16), ((16, E, E), BF16), ((2, E, E), F32), ((2, E + EXTRA, E), BF16)],
        [side1], own, other, cols, rows, flops=16 * 2 * E**3,
    )
    m1 = lax.ppermute(message, "seq", z_shift(2))
    m3 = lax.ppermute(message, "seq", z_shift(-2))
    m2 = lax.ppermute(message, "seq", z_shift(4))
    (part,) = call(local_kernel, [((16, BLK, E), F32)], [], proj, prefix, cols, rows, flops=16 * 6 * E**3)
    before, gone, row_message = call(
        row_kernel,
        [((2, E, E), F32), ((2, 8, E), F32), ((2, E + EXTRA, E), BF16)],
        [place1], total, message, m1, m2, m3,
    )
    earlier = [lax.ppermute(row_message, "seq", y_later(k)) for k in range(1, NY)]
    (flat,) = call(
        final_kernel, [((1024, 256), BF16)], [], *earlier, before, gone, part, proj, cols, starts, gain,
        flops=16 * 2 * E**3,
    )
    sent = lax.all_to_all(
        flat.reshape(16, 64, 256), ("seq", "head"), split_axis=0, concat_axis=0, tiled=True,
        axis_index_groups=OUT_GROUPS,
    )
    (out,) = call(order_kernel, [((64, 4096), BF16)], [], sent)
    return out


def solution(mesh):
    return jax.shard_map(
        on_device,
        mesh=mesh,
        in_specs=(P(("seq", "head"), None), P("seq", None, "head"), P("head", "seq"), P("head")),
        out_specs=P(("seq", "head"), None),
        check_vma=False,
    )
```

```python
import functools

import jax
import jax.numpy as jnp
from jax import lax
from jax.experimental import pallas as pl
from jax.experimental.pallas import tpu as pltpu
from jax.sharding import PartitionSpec as P

BLK = 128
E = 128
EPS = 1e-05
NY = 8
NZ = 8
NH = 8
EXTRA = 16
F32 = jnp.float32
BF16 = jnp.bfloat16
VMEM = pltpu.VMEM

Z_GROUPS = [[y * NZ + z for z in range(NZ)] for y in range(NY)]
ROW_GROUPS = [[y * NZ + p + 2 * i for i in range(4)] for y in range(NY) for p in range(2)]
OUT_GROUPS = [[g * 16 + i for i in range(16)] for g in range(NY * NZ // 2)]


def y_shift(d):
    return [(y * NZ + z, ((y + d) % NY) * NZ + z) for y in range(NY) for z in range(NZ)]


def y_later(d):
    return [(y * NZ + z, (y + d) * NZ + z) for y in range(NY - d) for z in range(NZ)]


PAIR = [(s, s ^ 1) for s in range(NY * NZ)]


def after(value, *earlier):
    return lax.optimization_barrier((value,) + earlier)[0]


def whole(count):
    return [pl.BlockSpec(memory_space=VMEM)] * count


def mm(a, b, dims=(((1,), (0,)), ((), ()))):
    return lax.dot_general(a, b, dims, preferred_element_type=F32)


def write_message(ref, head, state, decay):
    ref[head, :E, :] = state.astype(BF16)
    decay = jnp.broadcast_to(decay, (EXTRA, E))
    high = decay.astype(BF16)
    rest = decay - high.astype(F32)
    middle = rest.astype(BF16)
    low = (rest - middle.astype(F32)).astype(BF16)
    row = lax.broadcasted_iota(jnp.int32, (EXTRA, E), 0)
    part = jnp.where(row == 0, high.astype(F32), jnp.where(row == 1, middle.astype(F32), low.astype(F32)))
    ref[head, E:, :] = part.astype(BF16)


def read_decay(ref, head):
    rows = ref[head, E:, :].astype(F32)
    return (rows[0:1] + rows[1:2]) + rows[2:3]


def pieces_kernel(weight_ref, out_ref):
    for c in range(3):
        for i in range(NZ):
            half = slice((i % 2) * 256, (i % 2 + 1) * 256)
            out_ref[i, :, c * 256 : (c + 1) * 256] = weight_ref[c, :, half]


def order_kernel(sent_ref, out_ref):
    for s in range(2):
        for h in range(NH):
            out_ref[:, (h * 2 + s) * 256 : (h * 2 + s + 1) * 256] = sent_ref[s * NH + h]


def states_kernel(side_ref, own_ref, other_ref, col_ref, row_ref, proj_ref, prefix_ref, message_ref):
    side = side_ref[0]
    proj_ref[side] = own_ref[...].astype(BF16)
    proj_ref[1 - side] = other_ref[...].astype(BF16)
    for head in range(2):
        state = jnp.zeros((E, E), F32)
        decay = jnp.zeros((1, 1), F32)
        for n in range(8):
            at = head * 8 + n
            rows = slice((n % 4) * BLK, (n % 4 + 1) * BLK)
            keys = proj_ref[n // 4, rows, 256 + head * E : 256 + (head + 1) * E]
            values = proj_ref[n // 4, rows, 512 + head * E : 512 + (head + 1) * E]
            last = row_ref[at : at + 1, BLK - 1 : BLK]
            scale = jnp.exp(last - col_ref[:, at : at + 1])
            prefix_ref[at] = state.astype(BF16)
            scaled = (keys.astype(F32) * scale).astype(BF16)
            state = jnp.exp(last) * state + mm(scaled, values, (((0,), (0,)), ((), ())))
            decay = decay + last
        for copy in range(4):
            write_message(message_ref.at[copy], head, state, decay)


def local_kernel(proj_ref, prefix_ref, col_ref, row_ref, out_ref):
    causal = lax.broadcasted_iota(jnp.int32, (BLK, BLK), 0) >= lax.broadcasted_iota(jnp.int32, (BLK, BLK), 1)
    for head in range(2):
        for n in range(8):
            at = head * 8 + n
            rows = slice((n % 4) * BLK, (n % 4 + 1) * BLK)
            queries = proj_ref[n // 4, rows, head * E : (head + 1) * E]
            keys = proj_ref[n // 4, rows, 256 + head * E : 256 + (head + 1) * E]
            values = proj_ref[n // 4, rows, 512 + head * E : 512 + (head + 1) * E]
            col = col_ref[:, at : at + 1]
            gaps = col - row_ref[at : at + 1, :]
            weights = jnp.exp(jnp.where(causal, gaps, -1e30))
            scores = mm(queries, keys, (((1,), (1,)), ((), ()))) * weights
            scaled = (queries.astype(F32) * jnp.exp(col)).astype(BF16)
            out_ref[at] = mm(scores.astype(BF16), values) + mm(scaled, prefix_ref[at])


def row_kernel(place_ref, messages_ref, before_ref, decay_ref, message_ref):
    place = place_ref[0]
    for head in range(2):
        before = jnp.zeros((E, E), F32)
        total = jnp.zeros((E, E), F32)
        gone_before = jnp.zeros((1, E), F32)
        gone = jnp.zeros((1, E), F32)
        for k in (3, 2, 1, 0):
            block = messages_ref[k, head, :E, :].astype(F32)
            decay = read_decay(messages_ref.at[k], head)
            total = total + jnp.exp(gone) * block
            gone = gone + decay
            early = k < place
            before = before + jnp.where(early, jnp.exp(gone_before), 0.0) * block
            gone_before = gone_before + jnp.where(early, decay, 0.0)
        before_ref[head] = before
        decay_ref[head] = jnp.broadcast_to(gone_before, (8, E))
        write_message(message_ref, head, total, gone)


def final_kernel(*refs):
    messages = refs[:7]
    before_ref, decay_ref, part_ref, proj_ref, col_ref, start_ref, gain_ref, out_ref = refs[7:]
    for head in range(2):
        carried = jnp.zeros((E, E), F32)
        gone = jnp.zeros((1, E), F32)
        for ref in messages:
            carried = carried + jnp.exp(gone) * ref[head, :E, :].astype(F32)
            gone = gone + read_decay(ref, head)
        incoming = (jnp.exp(decay_ref[head, 0:1, :]) * carried + before_ref[head]).astype(BF16)
        gain = gain_ref[0:1, head * E : (head + 1) * E]
        for n in range(8):
            at = head * 8 + n
            rows = slice((n % 4) * BLK, (n % 4 + 1) * BLK)
            queries = proj_ref[n // 4, rows, head * E : (head + 1) * E]
            scale = jnp.exp(col_ref[:, at : at + 1] + start_ref[0:1, at : at + 1])
            scaled = (queries.astype(F32) * scale).astype(BF16)
            output = part_ref[at] + mm(scaled, incoming)
            meansq = jnp.mean(output * output, axis=1, keepdims=True)
            gained = output / jnp.sqrt(meansq + EPS) * gain
            out_ref[n * BLK : (n + 1) * BLK, head * E : (head + 1) * E] = gained.astype(BF16)


def call(kernel, outs, scalars, *args, flops=0):
    shapes = [jax.ShapeDtypeStruct(s, d) for s, d in outs]
    smem = [pl.BlockSpec(memory_space=pltpu.SMEM)] * len(scalars)
    moved = sum(a.size * a.dtype.itemsize for a in args)
    return pl.pallas_call(
        kernel,
        out_shape=shapes,
        in_specs=smem + whole(len(args)),
        out_specs=whole(len(outs)),
        cost_estimate=pl.CostEstimate(flops=flops, bytes_accessed=moved, transcendentals=0),
        compiler_params=pltpu.CompilerParams(vmem_limit_bytes=32 * 1024 * 1024),
    )(*scalars, *args)


def on_device(tokens, qkv_weight, log_decay, norm_gain):
    seq = lax.axis_index("seq")
    y, z = seq // NZ, seq % NZ
    side = z % 2
    place = z // 2
    side1 = side.reshape(1).astype(jnp.int32)
    place1 = place.reshape(1).astype(jnp.int32)

    (pieces,) = call(pieces_kernel, [((NZ, 48, 768), BF16)], [], qkv_weight.transpose(1, 0, 2))
    block = lax.all_to_all(pieces, "seq", split_axis=0, concat_axis=0, tiled=True, axis_index_groups=Z_GROUPS)

    own_rows = lax.all_gather(tokens, "head", axis=0, tiled=True)


    def add(total, tok, part, offset):
        x = lax.dynamic_slice_in_dim(tok, ((y + offset) % NY) * (NZ * 48), NZ * 48, 1)
        d = jnp.dot(x, part.reshape(NZ * 48, 768), preferred_element_type=F32)
        return d if total is None else total + d

    ups, downs = [block], [block]

    def hop(*earlier):
        ups.append(lax.ppermute(after(ups[-1], *earlier), "seq", y_shift(1)))
        downs.append(lax.ppermute(after(downs[-1], *earlier), "seq", y_shift(-1)))

    def add_step(total, tok, step):
        if step == 0:
            return add(total, tok, block, 0)
        return add(add(total, tok, ups[step], -step), tok, downs[step], step)

    hop()
    pair_tokens = lax.ppermute(after(tokens, block), "seq", PAIR)
    own = add_step(None, own_rows, 0)

    mine = lax.dynamic_slice_in_dim(log_decay, side * 2, 2, 0)
    wanted = lax.dynamic_slice_in_dim(log_decay, (1 - side) * 2, 2, 0)
    theirs = lax.ppermute(after(wanted, block), "seq", PAIR)
    both = jnp.where(side == 0, jnp.concatenate([mine, theirs], 1), jnp.concatenate([theirs, mine], 1))
    rows = jnp.cumsum(both.reshape(2, 8, BLK), axis=2)
    ends = rows[:, :, -1]
    starts = (jnp.cumsum(ends, axis=1) - ends).reshape(1, 16)
    rows = rows.reshape(16, BLK)
    cols = rows.T
    gain = lax.dynamic_slice_in_dim(norm_gain, side * 256, 256, 0).reshape(1, 256)

    first = (ups[1], downs[1], own, rows, cols, starts, gain)
    other_rows = lax.all_gather(after(pair_tokens, *first), "head", axis=0, tiled=True)
    hop()
    own = add_step(own, own_rows, 1)
    hop(own)
    own = add_step(own, own_rows, 2)
    up4 = lax.ppermute(after(ups[3], own)[:4], "seq", y_shift(1))
    down4 = lax.ppermute(after(downs[3], own)[4:], "seq", y_shift(-1))
    own = add_step(own, own_rows, 3)
    other = None
    for step in range(4):
        other = add_step(other, other_rows, step)
    up4, down4, own, other = lax.optimization_barrier((up4, down4, own, other))
    last = jnp.concatenate([up4, down4], 0)
    own = add(own, own_rows, last, 4)
    other = add(other, other_rows, last, 4)

    proj, prefix, messages = call(
        states_kernel,
        [((2, 512, 768), BF16), ((16, E, E), BF16), ((4, 2, E + EXTRA, E), BF16)],
        [side1], own, other, cols, rows, flops=16 * 2 * E**3,
    )
    messages = lax.all_to_all(messages, "seq", split_axis=0, concat_axis=0, tiled=True, axis_index_groups=ROW_GROUPS)
    (part,) = call(local_kernel, [((16, BLK, E), F32)], [], proj, prefix, cols, rows, flops=16 * 6 * E**3)
    before, gone, row_message = call(
        row_kernel,
        [((2, E, E), F32), ((2, 8, E), F32), ((2, E + EXTRA, E), BF16)],
        [place1], messages,
    )
    earlier = [lax.ppermute(row_message, "seq", y_later(k)) for k in range(1, NY)]
    (flat,) = call(
        final_kernel, [((1024, 256), BF16)], [], *earlier, before, gone, part, proj, cols, starts, gain,
        flops=16 * 2 * E**3,
    )
    sent = lax.all_to_all(
        flat.reshape(16, 64, 256), ("seq", "head"), split_axis=0, concat_axis=0, tiled=True,
        axis_index_groups=OUT_GROUPS,
    )
    (out,) = call(order_kernel, [((64, 4096), BF16)], [], sent)
    return out


def solution(mesh):
    return jax.shard_map(
        on_device,
        mesh=mesh,
        in_specs=(P(("seq", "head"), None), P("seq", None, "head"), P("head", "seq"), P("head")),
        out_specs=P(("seq", "head"), None),
        check_vma=False,
    )
```

```python
import functools

import jax
import jax.numpy as jnp
from jax import lax
from jax.experimental import pallas as pl
from jax.experimental.pallas import tpu as pltpu
from jax.sharding import PartitionSpec as P

BLK = 128
E = 128
EPS = 1e-05
NY = 8
NZ = 8
NH = 8
EXTRA = 16
F32 = jnp.float32
BF16 = jnp.bfloat16
VMEM = pltpu.VMEM

Z_GROUPS = [[y * NZ + z for z in range(NZ)] for y in range(NY)]
ROW_GROUPS = [[y * NZ + p + 2 * i for i in range(4)] for y in range(NY) for p in range(2)]
OUT_GROUPS = [[g * 16 + i for i in range(16)] for g in range(NY * NZ // 2)]


def y_shift(d):
    return [(y * NZ + z, ((y + d) % NY) * NZ + z) for y in range(NY) for z in range(NZ)]


def y_later(d):
    return [(y * NZ + z, (y + d) * NZ + z) for y in range(NY - d) for z in range(NZ)]


PAIR = [(s, s ^ 1) for s in range(NY * NZ)]


def after(value, *earlier):
    return lax.optimization_barrier((value,) + earlier)[0]


def whole(count):
    return [pl.BlockSpec(memory_space=VMEM)] * count


def mm(a, b, dims=(((1,), (0,)), ((), ()))):
    return lax.dot_general(a, b, dims, preferred_element_type=F32)


def write_message(ref, head, state, decay):
    ref[head, :E, :] = state.astype(BF16)
    decay = jnp.broadcast_to(decay, (EXTRA, E))
    high = decay.astype(BF16)
    rest = decay - high.astype(F32)
    middle = rest.astype(BF16)
    low = (rest - middle.astype(F32)).astype(BF16)
    row = lax.broadcasted_iota(jnp.int32, (EXTRA, E), 0)
    part = jnp.where(row == 0, high.astype(F32), jnp.where(row == 1, middle.astype(F32), low.astype(F32)))
    ref[head, E:, :] = part.astype(BF16)


def read_decay(ref, head):
    rows = ref[head, E:, :].astype(F32)
    return (rows[0:1] + rows[1:2]) + rows[2:3]


def pieces_kernel(weight_ref, out_ref):
    for c in range(3):
        for i in range(NZ):
            half = slice((i % 2) * 256, (i % 2 + 1) * 256)
            out_ref[i, :, c * 256 : (c + 1) * 256] = weight_ref[c, :, half]


def order_kernel(sent_ref, out_ref):
    for s in range(2):
        for h in range(NH):
            out_ref[:, (h * 2 + s) * 256 : (h * 2 + s + 1) * 256] = sent_ref[s * NH + h]


def states_kernel(total_ref, col_ref, row_ref, proj_ref, prefix_ref, message_ref):
    for half in range(2):
        proj_ref[half] = total_ref[half * 512 : (half + 1) * 512].astype(BF16)
    for head in range(2):
        state = jnp.zeros((E, E), F32)
        decay = jnp.zeros((1, 1), F32)
        for n in range(8):
            at = head * 8 + n
            rows = slice((n % 4) * BLK, (n % 4 + 1) * BLK)
            keys = proj_ref[n // 4, rows, 256 + head * E : 256 + (head + 1) * E]
            values = proj_ref[n // 4, rows, 512 + head * E : 512 + (head + 1) * E]
            last = row_ref[at : at + 1, BLK - 1 : BLK]
            scale = jnp.exp(last - col_ref[:, at : at + 1])
            prefix_ref[at] = state.astype(BF16)
            scaled = (keys.astype(F32) * scale).astype(BF16)
            state = jnp.exp(last) * state + mm(scaled, values, (((0,), (0,)), ((), ())))
            decay = decay + last
        for copy in range(4):
            write_message(message_ref.at[copy], head, state, decay)


def local_kernel(proj_ref, prefix_ref, col_ref, row_ref, out_ref):
    causal = lax.broadcasted_iota(jnp.int32, (BLK, BLK), 0) >= lax.broadcasted_iota(jnp.int32, (BLK, BLK), 1)
    for head in range(2):
        for n in range(8):
            at = head * 8 + n
            rows = slice((n % 4) * BLK, (n % 4 + 1) * BLK)
            queries = proj_ref[n // 4, rows, head * E : (head + 1) * E]
            keys = proj_ref[n // 4, rows, 256 + head * E : 256 + (head + 1) * E]
            values = proj_ref[n // 4, rows, 512 + head * E : 512 + (head + 1) * E]
            col = col_ref[:, at : at + 1]
            gaps = col - row_ref[at : at + 1, :]
            weights = jnp.exp(jnp.where(causal, gaps, -1e30))
            scores = mm(queries, keys, (((1,), (1,)), ((), ()))) * weights
            scaled = (queries.astype(F32) * jnp.exp(col)).astype(BF16)
            out_ref[at] = mm(scores.astype(BF16), values) + mm(scaled, prefix_ref[at])


def row_kernel(place_ref, messages_ref, before_ref, decay_ref, message_ref):
    place = place_ref[0]
    for head in range(2):
        before = jnp.zeros((E, E), F32)
        total = jnp.zeros((E, E), F32)
        gone_before = jnp.zeros((1, E), F32)
        gone = jnp.zeros((1, E), F32)
        for k in (3, 2, 1, 0):
            block = messages_ref[k, head, :E, :].astype(F32)
            decay = read_decay(messages_ref.at[k], head)
            total = total + jnp.exp(gone) * block
            gone = gone + decay
            early = k < place
            before = before + jnp.where(early, jnp.exp(gone_before), 0.0) * block
            gone_before = gone_before + jnp.where(early, decay, 0.0)
        before_ref[head] = before
        decay_ref[head] = jnp.broadcast_to(gone_before, (8, E))
        write_message(message_ref, head, total, gone)


def final_kernel(*refs):
    messages = refs[:7]
    before_ref, decay_ref, part_ref, proj_ref, col_ref, start_ref, gain_ref, out_ref = refs[7:]
    for head in range(2):
        carried = jnp.zeros((E, E), F32)
        gone = jnp.zeros((1, E), F32)
        for ref in messages:
            carried = carried + jnp.exp(gone) * ref[head, :E, :].astype(F32)
            gone = gone + read_decay(ref, head)
        incoming = (jnp.exp(decay_ref[head, 0:1, :]) * carried + before_ref[head]).astype(BF16)
        gain = gain_ref[0:1, head * E : (head + 1) * E]
        for n in range(8):
            at = head * 8 + n
            rows = slice((n % 4) * BLK, (n % 4 + 1) * BLK)
            queries = proj_ref[n // 4, rows, head * E : (head + 1) * E]
            scale = jnp.exp(col_ref[:, at : at + 1] + start_ref[0:1, at : at + 1])
            scaled = (queries.astype(F32) * scale).astype(BF16)
            output = part_ref[at] + mm(scaled, incoming)
            meansq = jnp.mean(output * output, axis=1, keepdims=True)
            gained = output / jnp.sqrt(meansq + EPS) * gain
            out_ref[n * BLK : (n + 1) * BLK, head * E : (head + 1) * E] = gained.astype(BF16)


def call(kernel, outs, scalars, *args, flops=0):
    shapes = [jax.ShapeDtypeStruct(s, d) for s, d in outs]
    smem = [pl.BlockSpec(memory_space=pltpu.SMEM)] * len(scalars)
    moved = sum(a.size * a.dtype.itemsize for a in args)
    return pl.pallas_call(
        kernel,
        out_shape=shapes,
        in_specs=smem + whole(len(args)),
        out_specs=whole(len(outs)),
        cost_estimate=pl.CostEstimate(flops=flops, bytes_accessed=moved, transcendentals=0),
        compiler_params=pltpu.CompilerParams(vmem_limit_bytes=32 * 1024 * 1024),
    )(*scalars, *args)


def on_device(tokens, qkv_weight, log_decay, norm_gain):
    seq = lax.axis_index("seq")
    y, z = seq // NZ, seq % NZ
    side = z % 2
    place = z // 2
    place1 = place.reshape(1).astype(jnp.int32)

    (pieces,) = call(pieces_kernel, [((NZ, 48, 768), BF16)], [], qkv_weight.transpose(1, 0, 2))
    block = lax.all_to_all(pieces, "seq", split_axis=0, concat_axis=0, tiled=True, axis_index_groups=Z_GROUPS)

    all_rows = lax.all_gather(tokens, ("seq", "head"), axis=0, tiled=True, axis_index_groups=OUT_GROUPS)


    def add(total, part, offset):
        x = lax.dynamic_slice_in_dim(all_rows, ((y + offset) % NY) * (NZ * 48), NZ * 48, 1)
        d = jnp.dot(x, part.reshape(NZ * 48, 768), preferred_element_type=F32)
        return d if total is None else total + d

    ups, downs = [block], [block]

    def hop(*earlier):
        ups.append(lax.ppermute(after(ups[-1], *earlier), "seq", y_shift(1)))
        downs.append(lax.ppermute(after(downs[-1], *earlier), "seq", y_shift(-1)))

    def add_step(total, step):
        return add(add(total, ups[step], -step), downs[step], step)

    hop()

    mine = lax.dynamic_slice_in_dim(log_decay, side * 2, 2, 0)
    wanted = lax.dynamic_slice_in_dim(log_decay, (1 - side) * 2, 2, 0)
    theirs = lax.ppermute(after(wanted, block), "seq", PAIR)
    both = jnp.where(side == 0, jnp.concatenate([mine, theirs], 1), jnp.concatenate([theirs, mine], 1))
    rows = jnp.cumsum(both.reshape(2, 8, BLK), axis=2)
    ends = rows[:, :, -1]
    starts = (jnp.cumsum(ends, axis=1) - ends).reshape(1, 16)
    rows = rows.reshape(16, BLK)
    cols = rows.T
    gain = lax.dynamic_slice_in_dim(norm_gain, side * 256, 256, 0).reshape(1, 256)

    hop()
    hop(all_rows, rows, cols, starts, gain)
    total = add_step(add(None, block, 0), 1)
    up4 = lax.ppermute(after(ups[3], total)[:4], "seq", y_shift(1))
    down4 = lax.ppermute(after(downs[3], total)[4:], "seq", y_shift(-1))
    total = add_step(add_step(total, 2), 3)
    up4, down4, total = lax.optimization_barrier((up4, down4, total))
    total = add(total, jnp.concatenate([up4, down4], 0), 4)

    proj, prefix, messages = call(
        states_kernel,
        [((2, 512, 768), BF16), ((16, E, E), BF16), ((4, 2, E + EXTRA, E), BF16)],
        [], total, cols, rows, flops=16 * 2 * E**3,
    )
    messages = lax.all_to_all(messages, "seq", split_axis=0, concat_axis=0, tiled=True, axis_index_groups=ROW_GROUPS)
    (part,) = call(local_kernel, [((16, BLK, E), F32)], [], proj, prefix, cols, rows, flops=16 * 6 * E**3)
    before, gone, row_message = call(
        row_kernel,
        [((2, E, E), F32), ((2, 8, E), F32), ((2, E + EXTRA, E), BF16)],
        [place1], messages,
    )
    earlier = [lax.ppermute(row_message, "seq", y_later(k)) for k in range(1, NY)]
    (flat,) = call(
        final_kernel, [((1024, 256), BF16)], [], *earlier, before, gone, part, proj, cols, starts, gain,
        flops=16 * 2 * E**3,
    )
    sent = lax.all_to_all(
        flat.reshape(16, 64, 256), ("seq", "head"), split_axis=0, concat_axis=0, tiled=True,
        axis_index_groups=OUT_GROUPS,
    )
    (out,) = call(order_kernel, [((64, 4096), BF16)], [], sent)
    return out


def solution(mesh):
    return jax.shard_map(
        on_device,
        mesh=mesh,
        in_specs=(P(("seq", "head"), None), P("seq", None, "head"), P("head", "seq"), P("head")),
        out_specs=P(("seq", "head"), None),
        check_vma=False,
    )
```

```python
import functools

import jax
import jax.numpy as jnp
from jax import lax
from jax.experimental import pallas as pl
from jax.experimental.pallas import tpu as pltpu
from jax.sharding import PartitionSpec as P

BLK = 128
E = 128
EPS = 1e-05
NY = 8
NZ = 8
NH = 8
EXTRA = 16
F32 = jnp.float32
BF16 = jnp.bfloat16
VMEM = pltpu.VMEM

Z_GROUPS = [[y * NZ + z for z in range(NZ)] for y in range(NY)]
Y_GROUPS = [[y * NZ + z for y in range(NY)] for z in range(NZ)]
ROW_GROUPS = [[y * NZ + p + 2 * i for i in range(4)] for y in range(NY) for p in range(2)]
OUT_GROUPS = [[g * 16 + i for i in range(16)] for g in range(NY * NZ // 2)]


def y_shift(d):
    return [(y * NZ + z, ((y + d) % NY) * NZ + z) for y in range(NY) for z in range(NZ)]


def y_later(d):
    return [(y * NZ + z, (y + d) * NZ + z) for y in range(NY - d) for z in range(NZ)]


PAIR = [(s, s ^ 1) for s in range(NY * NZ)]


def after(value, *earlier):
    return lax.optimization_barrier((value,) + earlier)[0]


def whole(count):
    return [pl.BlockSpec(memory_space=VMEM)] * count


def mm(a, b, dims=(((1,), (0,)), ((), ()))):
    return lax.dot_general(a, b, dims, preferred_element_type=F32)


def write_message(ref, head, state, decay):
    ref[head, :E, :] = state.astype(BF16)
    decay = jnp.broadcast_to(decay, (EXTRA, E))
    high = decay.astype(BF16)
    rest = decay - high.astype(F32)
    middle = rest.astype(BF16)
    low = (rest - middle.astype(F32)).astype(BF16)
    row = lax.broadcasted_iota(jnp.int32, (EXTRA, E), 0)
    part = jnp.where(row == 0, high.astype(F32), jnp.where(row == 1, middle.astype(F32), low.astype(F32)))
    ref[head, E:, :] = part.astype(BF16)


def read_decay(ref, head):
    rows = ref[head, E:, :].astype(F32)
    return (rows[0:1] + rows[1:2]) + rows[2:3]


def pieces_kernel(weight_ref, out_ref):
    for c in range(3):
        for i in range(NZ):
            half = slice((i % 2) * 256, (i % 2 + 1) * 256)
            out_ref[i, :, c * 256 : (c + 1) * 256] = weight_ref[c, :, half]


def order_kernel(sent_ref, out_ref):
    for s in range(2):
        for h in range(NH):
            out_ref[:, (h * 2 + s) * 256 : (h * 2 + s + 1) * 256] = sent_ref[s * NH + h]


def states_kernel(total_ref, col_ref, row_ref, proj_ref, prefix_ref, message_ref):
    for half in range(2):
        proj_ref[half] = total_ref[half * 512 : (half + 1) * 512].astype(BF16)
    for head in range(2):
        state = jnp.zeros((E, E), F32)
        decay = jnp.zeros((1, 1), F32)
        for n in range(8):
            at = head * 8 + n
            rows = slice((n % 4) * BLK, (n % 4 + 1) * BLK)
            keys = proj_ref[n // 4, rows, head * E : (head + 1) * E]
            values = proj_ref[n // 4, rows, 256 + head * E : 256 + (head + 1) * E]
            last = row_ref[at : at + 1, BLK - 1 : BLK]
            scale = jnp.exp(last - col_ref[:, at : at + 1])
            prefix_ref[at] = state.astype(BF16)
            scaled = (keys.astype(F32) * scale).astype(BF16)
            state = jnp.exp(last) * state + mm(scaled, values, (((0,), (0,)), ((), ())))
            decay = decay + last
        for copy in range(4):
            write_message(message_ref.at[copy], head, state, decay)


def local_kernel(total_ref, proj_ref, prefix_ref, col_ref, row_ref, query_ref, out_ref):
    for half in range(2):
        query_ref[half] = total_ref[half * 512 : (half + 1) * 512].astype(BF16)
    causal = lax.broadcasted_iota(jnp.int32, (BLK, BLK), 0) >= lax.broadcasted_iota(jnp.int32, (BLK, BLK), 1)
    for head in range(2):
        for n in range(8):
            at = head * 8 + n
            rows = slice((n % 4) * BLK, (n % 4 + 1) * BLK)
            queries = query_ref[n // 4, rows, head * E : (head + 1) * E]
            keys = proj_ref[n // 4, rows, head * E : (head + 1) * E]
            values = proj_ref[n // 4, rows, 256 + head * E : 256 + (head + 1) * E]
            col = col_ref[:, at : at + 1]
            gaps = col - row_ref[at : at + 1, :]
            weights = jnp.exp(jnp.where(causal, gaps, -1e30))
            scores = mm(queries, keys, (((1,), (1,)), ((), ()))) * weights
            scaled = (queries.astype(F32) * jnp.exp(col)).astype(BF16)
            out_ref[at] = mm(scores.astype(BF16), values) + mm(scaled, prefix_ref[at])


def row_kernel(place_ref, messages_ref, before_ref, decay_ref, message_ref):
    place = place_ref[0]
    for head in range(2):
        before = jnp.zeros((E, E), F32)
        total = jnp.zeros((E, E), F32)
        gone_before = jnp.zeros((1, E), F32)
        gone = jnp.zeros((1, E), F32)
        for k in (3, 2, 1, 0):
            block = messages_ref[k, head, :E, :].astype(F32)
            decay = read_decay(messages_ref.at[k], head)
            total = total + jnp.exp(gone) * block
            gone = gone + decay
            early = k < place
            before = before + jnp.where(early, jnp.exp(gone_before), 0.0) * block
            gone_before = gone_before + jnp.where(early, decay, 0.0)
        before_ref[head] = before
        decay_ref[head] = jnp.broadcast_to(gone_before, (8, E))
        write_message(message_ref, head, total, gone)


def final_kernel(*refs):
    messages = refs[:7]
    before_ref, decay_ref, part_ref, query_ref, col_ref, start_ref, gain_ref, out_ref = refs[7:]
    for head in range(2):
        carried = jnp.zeros((E, E), F32)
        gone = jnp.zeros((1, E), F32)
        for ref in messages:
            carried = carried + jnp.exp(gone) * ref[head, :E, :].astype(F32)
            gone = gone + read_decay(ref, head)
        incoming = (jnp.exp(decay_ref[head, 0:1, :]) * carried + before_ref[head]).astype(BF16)
        gain = gain_ref[0:1, head * E : (head + 1) * E]
        for n in range(8):
            at = head * 8 + n
            rows = slice((n % 4) * BLK, (n % 4 + 1) * BLK)
            queries = query_ref[n // 4, rows, head * E : (head + 1) * E]
            scale = jnp.exp(col_ref[:, at : at + 1] + start_ref[0:1, at : at + 1])
            scaled = (queries.astype(F32) * scale).astype(BF16)
            output = part_ref[at] + mm(scaled, incoming)
            meansq = jnp.mean(output * output, axis=1, keepdims=True)
            gained = output / jnp.sqrt(meansq + EPS) * gain
            out_ref[n * BLK : (n + 1) * BLK, head * E : (head + 1) * E] = gained.astype(BF16)


def call(kernel, outs, scalars, *args, flops=0):
    shapes = [jax.ShapeDtypeStruct(s, d) for s, d in outs]
    smem = [pl.BlockSpec(memory_space=pltpu.SMEM)] * len(scalars)
    moved = sum(a.size * a.dtype.itemsize for a in args)
    return pl.pallas_call(
        kernel,
        out_shape=shapes,
        in_specs=smem + whole(len(args)),
        out_specs=whole(len(outs)),
        cost_estimate=pl.CostEstimate(flops=flops, bytes_accessed=moved, transcendentals=0),
        compiler_params=pltpu.CompilerParams(vmem_limit_bytes=32 * 1024 * 1024),
    )(*scalars, *args)


def on_device(tokens, qkv_weight, log_decay, norm_gain):
    seq = lax.axis_index("seq")
    y, z = seq // NZ, seq % NZ
    side = z % 2
    place = z // 2
    place1 = place.reshape(1).astype(jnp.int32)

    (pieces,) = call(pieces_kernel, [((NZ, 48, 768), BF16)], [], qkv_weight.transpose(1, 0, 2))
    block = lax.all_to_all(pieces, "seq", split_axis=0, concat_axis=0, tiled=True, axis_index_groups=Z_GROUPS)

    all_rows = lax.all_gather(tokens, ("seq", "head"), axis=0, tiled=True, axis_index_groups=OUT_GROUPS)


    def add(total, part, offset):
        x = lax.dynamic_slice_in_dim(all_rows, ((y + offset) % NY) * (NZ * 48), NZ * 48, 1)
        d = jnp.dot(x, part.reshape(NZ * 48, 512), preferred_element_type=F32)
        return d if total is None else total + d

    query_block = block[:, :, :256]
    block = block[:, :, 256:]
    ups, downs = [block], [block]

    def hop(*earlier):
        ups.append(lax.ppermute(after(ups[-1], *earlier), "seq", y_shift(1)))
        downs.append(lax.ppermute(after(downs[-1], *earlier), "seq", y_shift(-1)))

    def add_step(total, step):
        return add(add(total, ups[step], -step), downs[step], step)

    hop()

    mine = lax.dynamic_slice_in_dim(log_decay, side * 2, 2, 0)
    wanted = lax.dynamic_slice_in_dim(log_decay, (1 - side) * 2, 2, 0)
    theirs = lax.ppermute(after(wanted, block), "seq", PAIR)
    both = jnp.where(side == 0, jnp.concatenate([mine, theirs], 1), jnp.concatenate([theirs, mine], 1))
    rows = jnp.cumsum(both.reshape(2, 8, BLK), axis=2)
    ends = rows[:, :, -1]
    starts = (jnp.cumsum(ends, axis=1) - ends).reshape(1, 16)
    rows = rows.reshape(16, BLK)
    cols = rows.T
    gain = lax.dynamic_slice_in_dim(norm_gain, side * 256, 256, 0).reshape(1, 256)

    hop()
    hop(rows, cols, starts, gain)
    total = add(add(None, block, 0), ups[1], -1)
    query_weight = lax.all_gather(
        after(query_block, all_rows), "seq", axis=0, tiled=True, axis_index_groups=Y_GROUPS
    ).reshape(NY * NZ * 48, 256)
    up4 = lax.ppermute(after(ups[3], total)[:4], "seq", y_shift(1))
    down4 = lax.ppermute(after(downs[3], total)[4:], "seq", y_shift(-1))
    total = add_step(add_step(add(total, downs[1], 1), 2), 3)
    up4, down4, total = lax.optimization_barrier((up4, down4, total))
    total = add(total, jnp.concatenate([up4, down4], 0), 4)

    proj, prefix, messages = call(
        states_kernel,
        [((2, 512, 512), BF16), ((16, E, E), BF16), ((4, 2, E + EXTRA, E), BF16)],
        [], total, cols, rows, flops=16 * 2 * E**3,
    )
    messages = lax.all_to_all(messages, "seq", split_axis=0, concat_axis=0, tiled=True, axis_index_groups=ROW_GROUPS)
    query_total = jnp.dot(all_rows, after(query_weight, messages), preferred_element_type=F32)
    query, part = call(
        local_kernel, [((2, 512, 256), BF16), ((16, BLK, E), F32)], [], query_total, proj, prefix, cols, rows,
        flops=16 * 6 * E**3,
    )
    before, gone, row_message = call(
        row_kernel,
        [((2, E, E), F32), ((2, 8, E), F32), ((2, E + EXTRA, E), BF16)],
        [place1], messages,
    )
    earlier = [lax.ppermute(row_message, "seq", y_later(k)) for k in range(1, NY)]
    (flat,) = call(
        final_kernel, [((1024, 256), BF16)], [], *earlier, before, gone, part, query, cols, starts, gain,
        flops=16 * 2 * E**3,
    )
    sent = lax.all_to_all(
        flat.reshape(16, 64, 256), ("seq", "head"), split_axis=0, concat_axis=0, tiled=True,
        axis_index_groups=OUT_GROUPS,
    )
    (out,) = call(order_kernel, [((64, 4096), BF16)], [], sent)
    return out


def solution(mesh):
    return jax.shard_map(
        on_device,
        mesh=mesh,
        in_specs=(P(("seq", "head"), None), P("seq", None, "head"), P("head", "seq"), P("head")),
        out_specs=P(("seq", "head"), None),
        check_vma=False,
    )
```

```python
import functools

import jax
import jax.numpy as jnp
from jax import lax
from jax.experimental import pallas as pl
from jax.experimental.pallas import tpu as pltpu
from jax.sharding import PartitionSpec as P

BLK = 128
E = 128
EPS = 1e-05
NY = 8
NZ = 8
NH = 8
EXTRA = 16
F32 = jnp.float32
BF16 = jnp.bfloat16
VMEM = pltpu.VMEM

Z_GROUPS = [[y * NZ + z for z in range(NZ)] for y in range(NY)]
Y_GROUPS = [[y * NZ + z for y in range(NY)] for z in range(NZ)]
ROW_GROUPS = [[y * NZ + p + 2 * i for i in range(4)] for y in range(NY) for p in range(2)]
OUT_GROUPS = [[g * 16 + i for i in range(16)] for g in range(NY * NZ // 2)]


def y_shift(d):
    return [(y * NZ + z, ((y + d) % NY) * NZ + z) for y in range(NY) for z in range(NZ)]


def y_later(d):
    return [(y * NZ + z, (y + d) * NZ + z) for y in range(NY - d) for z in range(NZ)]


PAIR = [(s, s ^ 1) for s in range(NY * NZ)]


def after(value, *earlier):
    return lax.optimization_barrier((value,) + earlier)[0]


def whole(count):
    return [pl.BlockSpec(memory_space=VMEM)] * count


def mm(a, b, dims=(((1,), (0,)), ((), ()))):
    return lax.dot_general(a, b, dims, preferred_element_type=F32)


def write_message(ref, head, state, decay):
    ref[head, :E, :] = state.astype(BF16)
    decay = jnp.broadcast_to(decay, (EXTRA, E))
    high = decay.astype(BF16)
    rest = decay - high.astype(F32)
    middle = rest.astype(BF16)
    low = (rest - middle.astype(F32)).astype(BF16)
    row = lax.broadcasted_iota(jnp.int32, (EXTRA, E), 0)
    part = jnp.where(row == 0, high.astype(F32), jnp.where(row == 1, middle.astype(F32), low.astype(F32)))
    ref[head, E:, :] = part.astype(BF16)


def read_decay(ref, head):
    rows = ref[head, E:, :].astype(F32)
    return (rows[0:1] + rows[1:2]) + rows[2:3]


def pieces_kernel(weight_ref, query_ref, out_ref):
    for i in range(NZ):
        half = slice((i % 2) * 256, (i % 2 + 1) * 256)
        query_ref[i] = weight_ref[0, :, half]
        for c in range(2):
            out_ref[i, :, c * 256 : (c + 1) * 256] = weight_ref[c + 1, :, half]


def order_kernel(sent_ref, out_ref):
    for s in range(2):
        for h in range(NH):
            out_ref[:, (h * 2 + s) * 256 : (h * 2 + s + 1) * 256] = sent_ref[s * NH + h]


def states_kernel(total_ref, last_ref, col_ref, row_ref, proj_ref, prefix_ref, message_ref):
    for half in range(2):
        part = slice(half * 512, (half + 1) * 512)
        proj_ref[half] = (total_ref[part] + last_ref[part]).astype(BF16)
    for head in range(2):
        state = jnp.zeros((E, E), F32)
        decay = jnp.zeros((1, 1), F32)
        for n in range(8):
            at = head * 8 + n
            rows = slice((n % 4) * BLK, (n % 4 + 1) * BLK)
            keys = proj_ref[n // 4, rows, head * E : (head + 1) * E]
            values = proj_ref[n // 4, rows, 256 + head * E : 256 + (head + 1) * E]
            last = row_ref[at : at + 1, BLK - 1 : BLK]
            scale = jnp.exp(last - col_ref[:, at : at + 1])
            prefix_ref[at] = state.astype(BF16)
            scaled = (keys.astype(F32) * scale).astype(BF16)
            state = jnp.exp(last) * state + mm(scaled, values, (((0,), (0,)), ((), ())))
            decay = decay + last
        for copy in range(4):
            write_message(message_ref.at[copy], head, state, decay)


def local_kernel(total_ref, proj_ref, prefix_ref, col_ref, row_ref, query_ref, out_ref):
    for half in range(2):
        query_ref[half] = total_ref[half * 512 : (half + 1) * 512].astype(BF16)
    causal = lax.broadcasted_iota(jnp.int32, (BLK, BLK), 0) >= lax.broadcasted_iota(jnp.int32, (BLK, BLK), 1)
    for head in range(2):
        for n in range(8):
            at = head * 8 + n
            rows = slice((n % 4) * BLK, (n % 4 + 1) * BLK)
            queries = query_ref[n // 4, rows, head * E : (head + 1) * E]
            keys = proj_ref[n // 4, rows, head * E : (head + 1) * E]
            values = proj_ref[n // 4, rows, 256 + head * E : 256 + (head + 1) * E]
            col = col_ref[:, at : at + 1]
            gaps = col - row_ref[at : at + 1, :]
            weights = jnp.exp(jnp.where(causal, gaps, -1e30))
            scores = mm(queries, keys, (((1,), (1,)), ((), ()))) * weights
            scaled = (queries.astype(F32) * jnp.exp(col)).astype(BF16)
            out_ref[at] = mm(scores.astype(BF16), values) + mm(scaled, prefix_ref[at])


def row_kernel(place_ref, messages_ref, before_ref, decay_ref, message_ref):
    place = place_ref[0]
    for head in range(2):
        before = jnp.zeros((E, E), F32)
        total = jnp.zeros((E, E), F32)
        gone_before = jnp.zeros((1, E), F32)
        gone = jnp.zeros((1, E), F32)
        for k in (3, 2, 1, 0):
            block = messages_ref[k, head, :E, :].astype(F32)
            decay = read_decay(messages_ref.at[k], head)
            total = total + jnp.exp(gone) * block
            gone = gone + decay
            early = k < place
            before = before + jnp.where(early, jnp.exp(gone_before), 0.0) * block
            gone_before = gone_before + jnp.where(early, decay, 0.0)
        before_ref[head] = before
        decay_ref[head] = jnp.broadcast_to(gone_before, (8, E))
        write_message(message_ref, head, total, gone)


def final_kernel(*refs):
    messages = refs[:7]
    before_ref, decay_ref, part_ref, query_ref, col_ref, start_ref, gain_ref, out_ref = refs[7:]
    for head in range(2):
        carried = jnp.zeros((E, E), F32)
        gone = jnp.zeros((1, E), F32)
        for ref in messages:
            carried = carried + jnp.exp(gone) * ref[head, :E, :].astype(F32)
            gone = gone + read_decay(ref, head)
        incoming = (jnp.exp(decay_ref[head, 0:1, :]) * carried + before_ref[head]).astype(BF16)
        gain = gain_ref[0:1, head * E : (head + 1) * E]
        for n in range(8):
            at = head * 8 + n
            rows = slice((n % 4) * BLK, (n % 4 + 1) * BLK)
            queries = query_ref[n // 4, rows, head * E : (head + 1) * E]
            scale = jnp.exp(col_ref[:, at : at + 1] + start_ref[0:1, at : at + 1])
            scaled = (queries.astype(F32) * scale).astype(BF16)
            output = part_ref[at] + mm(scaled, incoming)
            meansq = jnp.mean(output * output, axis=1, keepdims=True)
            gained = output / jnp.sqrt(meansq + EPS) * gain
            out_ref[n * BLK : (n + 1) * BLK, head * E : (head + 1) * E] = gained.astype(BF16)


def call(kernel, outs, scalars, *args, flops=0):
    shapes = [jax.ShapeDtypeStruct(s, d) for s, d in outs]
    smem = [pl.BlockSpec(memory_space=pltpu.SMEM)] * len(scalars)
    moved = sum(a.size * a.dtype.itemsize for a in args)
    return pl.pallas_call(
        kernel,
        out_shape=shapes,
        in_specs=smem + whole(len(args)),
        out_specs=whole(len(outs)),
        cost_estimate=pl.CostEstimate(flops=flops, bytes_accessed=moved, transcendentals=0),
        compiler_params=pltpu.CompilerParams(vmem_limit_bytes=32 * 1024 * 1024),
    )(*scalars, *args)


def on_device(tokens, qkv_weight, log_decay, norm_gain):
    seq = lax.axis_index("seq")
    y, z = seq // NZ, seq % NZ
    side = z % 2
    place = z // 2
    place1 = place.reshape(1).astype(jnp.int32)

    query_pieces, pieces = call(
        pieces_kernel, [((NZ, 48, 256), BF16), ((NZ, 48, 512), BF16)], [], qkv_weight.transpose(1, 0, 2)
    )
    block = lax.all_to_all(pieces, "seq", split_axis=0, concat_axis=0, tiled=True, axis_index_groups=Z_GROUPS)

    all_rows = lax.all_gather(tokens, ("seq", "head"), axis=0, tiled=True, axis_index_groups=OUT_GROUPS)


    def add(total, part, offset):
        x = lax.dynamic_slice_in_dim(all_rows, ((y + offset) % NY) * (NZ * 48), NZ * 48, 1)
        d = jnp.dot(x, part.reshape(NZ * 48, 512), preferred_element_type=F32)
        return d if total is None else total + d

    ups, downs = [block], [block]

    def hop(*earlier):
        ups.append(lax.ppermute(after(ups[-1], *earlier), "seq", y_shift(1)))
        downs.append(lax.ppermute(after(downs[-1], *earlier), "seq", y_shift(-1)))

    def add_step(total, step):
        return add(add(total, ups[step], -step), downs[step], step)

    hop()
    query_block = lax.all_to_all(
        after(query_pieces, block), "seq", split_axis=0, concat_axis=0, tiled=True, axis_index_groups=Z_GROUPS
    )

    mine = lax.dynamic_slice_in_dim(log_decay, side * 2, 2, 0)
    wanted = lax.dynamic_slice_in_dim(log_decay, (1 - side) * 2, 2, 0)
    theirs = lax.ppermute(after(wanted, block), "seq", PAIR)
    both = jnp.where(side == 0, jnp.concatenate([mine, theirs], 1), jnp.concatenate([theirs, mine], 1))
    rows = jnp.cumsum(both.reshape(2, 8, BLK), axis=2)
    ends = rows[:, :, -1]
    starts = (jnp.cumsum(ends, axis=1) - ends).reshape(1, 16)
    rows = rows.reshape(16, BLK)
    cols = rows.T
    gain = lax.dynamic_slice_in_dim(norm_gain, side * 256, 256, 0).reshape(1, 256)

    hop()
    hop(rows, cols, starts, gain)
    total = add(add(None, block, 0), ups[1], -1)
    query_weight = lax.all_gather(
        after(query_block, all_rows), "seq", axis=0, tiled=True, axis_index_groups=Y_GROUPS
    ).reshape(NY * NZ * 48, 256)
    up4 = lax.ppermute(after(ups[3], total)[:4], "seq", y_shift(1))
    down4 = lax.ppermute(after(downs[3], total)[4:], "seq", y_shift(-1))
    total = add_step(add_step(add(total, downs[1], 1), 2), 3)
    up4, down4, total = lax.optimization_barrier((up4, down4, total))
    last = add(None, jnp.concatenate([up4, down4], 0), 4)

    proj, prefix, messages = call(
        states_kernel,
        [((2, 512, 512), BF16), ((16, E, E), BF16), ((4, 2, E + EXTRA, E), BF16)],
        [], total, last, cols, rows, flops=16 * 2 * E**3,
    )
    messages = lax.all_to_all(messages, "seq", split_axis=0, concat_axis=0, tiled=True, axis_index_groups=ROW_GROUPS)
    query_total = jnp.dot(all_rows, after(query_weight, messages), preferred_element_type=F32)
    query, part = call(
        local_kernel, [((2, 512, 256), BF16), ((16, BLK, E), F32)], [], query_total, proj, prefix, cols, rows,
        flops=16 * 6 * E**3,
    )
    before, gone, row_message = call(
        row_kernel,
        [((2, E, E), F32), ((2, 8, E), F32), ((2, E + EXTRA, E), BF16)],
        [place1], messages,
    )
    earlier = [lax.ppermute(row_message, "seq", y_later(k)) for k in range(1, NY)]
    (flat,) = call(
        final_kernel, [((1024, 256), BF16)], [], *earlier, before, gone, part, query, cols, starts, gain,
        flops=16 * 2 * E**3,
    )
    sent = lax.all_to_all(
        flat.reshape(16, 64, 256), ("seq", "head"), split_axis=0, concat_axis=0, tiled=True,
        axis_index_groups=OUT_GROUPS,
    )
    (out,) = call(order_kernel, [((64, 4096), BF16)], [], sent)
    return out


def solution(mesh):
    return jax.shard_map(
        on_device,
        mesh=mesh,
        in_specs=(P(("seq", "head"), None), P("seq", None, "head"), P("head", "seq"), P("head")),
        out_specs=P(("seq", "head"), None),
        check_vma=False,
    )
```

```python
import functools

import jax
import jax.numpy as jnp
from jax import lax
from jax.experimental import pallas as pl
from jax.experimental.pallas import tpu as pltpu
from jax.sharding import PartitionSpec as P

BLK = 128
E = 128
EPS = 1e-05
NY = 8
NZ = 8
NH = 8
EXTRA = 16
F32 = jnp.float32
BF16 = jnp.bfloat16
VMEM = pltpu.VMEM

Z_GROUPS = [[y * NZ + z for z in range(NZ)] for y in range(NY)]
Y_GROUPS = [[y * NZ + z for y in range(NY)] for z in range(NZ)]
ROW_GROUPS = [[y * NZ + p + 2 * i for i in range(4)] for y in range(NY) for p in range(2)]
OUT_GROUPS = [[g * 16 + i for i in range(16)] for g in range(NY * NZ // 2)]


def y_shift(d):
    return [(y * NZ + z, ((y + d) % NY) * NZ + z) for y in range(NY) for z in range(NZ)]


def y_later(d):
    return [(y * NZ + z, (y + d) * NZ + z) for y in range(NY - d) for z in range(NZ)]


PAIR = [(s, s ^ 1) for s in range(NY * NZ)]


def after(value, *earlier):
    return lax.optimization_barrier((value,) + earlier)[0]


def whole(count):
    return [pl.BlockSpec(memory_space=VMEM)] * count


def mm(a, b, dims=(((1,), (0,)), ((), ()))):
    return lax.dot_general(a, b, dims, preferred_element_type=F32)


def write_message(ref, head, state, decay):
    ref[head, :E, :] = state.astype(BF16)
    decay = jnp.broadcast_to(decay, (EXTRA, E))
    high = decay.astype(BF16)
    rest = decay - high.astype(F32)
    middle = rest.astype(BF16)
    low = (rest - middle.astype(F32)).astype(BF16)
    row = lax.broadcasted_iota(jnp.int32, (EXTRA, E), 0)
    part = jnp.where(row == 0, high.astype(F32), jnp.where(row == 1, middle.astype(F32), low.astype(F32)))
    ref[head, E:, :] = part.astype(BF16)


def read_decay(ref, head):
    rows = ref[head, E:, :].astype(F32)
    return (rows[0:1] + rows[1:2]) + rows[2:3]


def pieces_kernel(weight_ref, out_ref):
    for c in range(3):
        for i in range(NZ):
            half = slice((i % 2) * 256, (i % 2 + 1) * 256)
            out_ref[i, :, c * 256 : (c + 1) * 256] = weight_ref[c, :, half]


def order_kernel(sent_ref, out_ref):
    for s in range(2):
        for h in range(NH):
            out_ref[:, (h * 2 + s) * 256 : (h * 2 + s + 1) * 256] = sent_ref[s * NH + h]


def states_kernel(total_ref, last_ref, col_ref, row_ref, proj_ref, prefix_ref, message_ref):
    for half in range(2):
        part = slice(half * 512, (half + 1) * 512)
        proj_ref[half] = (total_ref[part] + last_ref[part]).astype(BF16)
    for head in range(2):
        state = jnp.zeros((E, E), F32)
        decay = jnp.zeros((1, 1), F32)
        for n in range(8):
            at = head * 8 + n
            rows = slice((n % 4) * BLK, (n % 4 + 1) * BLK)
            keys = proj_ref[n // 4, rows, head * E : (head + 1) * E]
            values = proj_ref[n // 4, rows, 256 + head * E : 256 + (head + 1) * E]
            last = row_ref[at : at + 1, BLK - 1 : BLK]
            scale = jnp.exp(last - col_ref[:, at : at + 1])
            prefix_ref[at] = state.astype(BF16)
            scaled = (keys.astype(F32) * scale).astype(BF16)
            state = jnp.exp(last) * state + mm(scaled, values, (((0,), (0,)), ((), ())))
            decay = decay + last
        for copy in range(4):
            write_message(message_ref.at[copy], head, state, decay)


def local_kernel(total_ref, proj_ref, prefix_ref, col_ref, row_ref, query_ref, out_ref):
    for half in range(2):
        query_ref[half] = total_ref[half * 512 : (half + 1) * 512].astype(BF16)
    causal = lax.broadcasted_iota(jnp.int32, (BLK, BLK), 0) >= lax.broadcasted_iota(jnp.int32, (BLK, BLK), 1)
    for head in range(2):
        for n in range(8):
            at = head * 8 + n
            rows = slice((n % 4) * BLK, (n % 4 + 1) * BLK)
            queries = query_ref[n // 4, rows, head * E : (head + 1) * E]
            keys = proj_ref[n // 4, rows, head * E : (head + 1) * E]
            values = proj_ref[n // 4, rows, 256 + head * E : 256 + (head + 1) * E]
            col = col_ref[:, at : at + 1]
            gaps = col - row_ref[at : at + 1, :]
            weights = jnp.exp(jnp.where(causal, gaps, -1e30))
            scores = mm(queries, keys, (((1,), (1,)), ((), ()))) * weights
            scaled = (queries.astype(F32) * jnp.exp(col)).astype(BF16)
            out_ref[at] = mm(scores.astype(BF16), values) + mm(scaled, prefix_ref[at])


def row_kernel(place_ref, messages_ref, before_ref, decay_ref, message_ref):
    place = place_ref[0]
    for head in range(2):
        before = jnp.zeros((E, E), F32)
        total = jnp.zeros((E, E), F32)
        gone_before = jnp.zeros((1, E), F32)
        gone = jnp.zeros((1, E), F32)
        for k in (3, 2, 1, 0):
            block = messages_ref[k, head, :E, :].astype(F32)
            decay = read_decay(messages_ref.at[k], head)
            total = total + jnp.exp(gone) * block
            gone = gone + decay
            early = k < place
            before = before + jnp.where(early, jnp.exp(gone_before), 0.0) * block
            gone_before = gone_before + jnp.where(early, decay, 0.0)
        before_ref[head] = before
        decay_ref[head] = jnp.broadcast_to(gone_before, (8, E))
        write_message(message_ref, head, total, gone)


def final_kernel(*refs):
    messages = refs[:7]
    before_ref, decay_ref, part_ref, query_ref, col_ref, start_ref, gain_ref, out_ref = refs[7:]
    for head in range(2):
        carried = jnp.zeros((E, E), F32)
        gone = jnp.zeros((1, E), F32)
        for ref in messages:
            carried = carried + jnp.exp(gone) * ref[head, :E, :].astype(F32)
            gone = gone + read_decay(ref, head)
        incoming = (jnp.exp(decay_ref[head, 0:1, :]) * carried + before_ref[head]).astype(BF16)
        gain = gain_ref[0:1, head * E : (head + 1) * E]
        for n in range(8):
            at = head * 8 + n
            rows = slice((n % 4) * BLK, (n % 4 + 1) * BLK)
            queries = query_ref[n // 4, rows, head * E : (head + 1) * E]
            scale = jnp.exp(col_ref[:, at : at + 1] + start_ref[0:1, at : at + 1])
            scaled = (queries.astype(F32) * scale).astype(BF16)
            output = part_ref[at] + mm(scaled, incoming)
            meansq = jnp.mean(output * output, axis=1, keepdims=True)
            gained = output / jnp.sqrt(meansq + EPS) * gain
            out_ref[n * BLK : (n + 1) * BLK, head * E : (head + 1) * E] = gained.astype(BF16)


def call(kernel, outs, scalars, *args, flops=0):
    shapes = [jax.ShapeDtypeStruct(s, d) for s, d in outs]
    smem = [pl.BlockSpec(memory_space=pltpu.SMEM)] * len(scalars)
    moved = sum(a.size * a.dtype.itemsize for a in args)
    return pl.pallas_call(
        kernel,
        out_shape=shapes,
        in_specs=smem + whole(len(args)),
        out_specs=whole(len(outs)),
        cost_estimate=pl.CostEstimate(flops=flops, bytes_accessed=moved, transcendentals=0),
        compiler_params=pltpu.CompilerParams(vmem_limit_bytes=32 * 1024 * 1024),
    )(*scalars, *args)


def on_device(tokens, qkv_weight, log_decay, norm_gain):
    seq = lax.axis_index("seq")
    y, z = seq // NZ, seq % NZ
    side = z % 2
    place = z // 2
    place1 = place.reshape(1).astype(jnp.int32)

    (pieces,) = call(pieces_kernel, [((NZ, 48, 768), BF16)], [], qkv_weight.transpose(1, 0, 2))
    block = lax.all_to_all(pieces, "seq", split_axis=0, concat_axis=0, tiled=True, axis_index_groups=Z_GROUPS)

    all_rows = lax.all_gather(tokens, ("seq", "head"), axis=0, tiled=True, axis_index_groups=OUT_GROUPS)


    def add(total, part, offset):
        x = lax.dynamic_slice_in_dim(all_rows, ((y + offset) % NY) * (NZ * 48), NZ * 48, 1)
        d = jnp.dot(x, part.reshape(NZ * 48, 512), preferred_element_type=F32)
        return d if total is None else total + d

    mine = lax.dynamic_slice_in_dim(log_decay, side * 2, 2, 0)
    wanted = lax.dynamic_slice_in_dim(log_decay, (1 - side) * 2, 2, 0)
    theirs = lax.ppermute(wanted, "seq", PAIR)
    both = jnp.where(side == 0, jnp.concatenate([mine, theirs], 1), jnp.concatenate([theirs, mine], 1))
    rows = jnp.cumsum(both.reshape(2, 8, BLK), axis=2)
    ends = rows[:, :, -1]
    starts = (jnp.cumsum(ends, axis=1) - ends).reshape(1, 16)
    rows = rows.reshape(16, BLK)
    cols = rows.T
    gain = lax.dynamic_slice_in_dim(norm_gain, side * 256, 256, 0).reshape(1, 256)

    block, rows, cols, starts, gain = lax.optimization_barrier((block, rows, cols, starts, gain))
    query_block = block[:, :, :256]
    block = block[:, :, 256:]
    ups, downs = [block], [block]

    def hop(*earlier):
        ups.append(lax.ppermute(after(ups[-1], *earlier), "seq", y_shift(1)))
        downs.append(lax.ppermute(after(downs[-1], *earlier), "seq", y_shift(-1)))

    def add_step(total, step):
        return add(add(total, ups[step], -step), downs[step], step)

    hop()

    hop()
    hop()
    total = add(add(None, block, 0), ups[1], -1)
    query_weight = lax.all_gather(
        after(query_block, all_rows), "seq", axis=0, tiled=True, axis_index_groups=Y_GROUPS
    ).reshape(NY * NZ * 48, 256)
    up4 = lax.ppermute(after(ups[3], total)[:4], "seq", y_shift(1))
    down4 = lax.ppermute(after(downs[3], total)[4:], "seq", y_shift(-1))
    total = add_step(add_step(add(total, downs[1], 1), 2), 3)
    up4, down4, total = lax.optimization_barrier((up4, down4, total))
    last = add(None, jnp.concatenate([up4, down4], 0), 4)

    proj, prefix, messages = call(
        states_kernel,
        [((2, 512, 512), BF16), ((16, E, E), BF16), ((4, 2, E + EXTRA, E), BF16)],
        [], total, last, cols, rows, flops=16 * 2 * E**3,
    )
    messages = lax.all_to_all(messages, "seq", split_axis=0, concat_axis=0, tiled=True, axis_index_groups=ROW_GROUPS)
    query_total = jnp.dot(all_rows, after(query_weight, messages), preferred_element_type=F32)
    query, part = call(
        local_kernel, [((2, 512, 256), BF16), ((16, BLK, E), F32)], [], query_total, proj, prefix, cols, rows,
        flops=16 * 6 * E**3,
    )
    before, gone, row_message = call(
        row_kernel,
        [((2, E, E), F32), ((2, 8, E), F32), ((2, E + EXTRA, E), BF16)],
        [place1], messages,
    )
    earlier = [lax.ppermute(row_message, "seq", y_later(k)) for k in range(1, NY)]
    (flat,) = call(
        final_kernel, [((1024, 256), BF16)], [], *earlier, before, gone, part, query, cols, starts, gain,
        flops=16 * 2 * E**3,
    )
    sent = lax.all_to_all(
        flat.reshape(16, 64, 256), ("seq", "head"), split_axis=0, concat_axis=0, tiled=True,
        axis_index_groups=OUT_GROUPS,
    )
    (out,) = call(order_kernel, [((64, 4096), BF16)], [], sent)
    return out


def solution(mesh):
    return jax.shard_map(
        on_device,
        mesh=mesh,
        in_specs=(P(("seq", "head"), None), P("seq", None, "head"), P("head", "seq"), P("head")),
        out_specs=P(("seq", "head"), None),
        check_vma=False,
    )
```

```python
import functools

import jax
import jax.numpy as jnp
from jax import lax
from jax.experimental import pallas as pl
from jax.experimental.pallas import tpu as pltpu
from jax.sharding import PartitionSpec as P

BLK = 128
E = 128
EPS = 1e-05
NY = 8
NZ = 8
NH = 8
EXTRA = 16
F32 = jnp.float32
BF16 = jnp.bfloat16
VMEM = pltpu.VMEM

Z_GROUPS = [[y * NZ + z for z in range(NZ)] for y in range(NY)]
Y_GROUPS = [[y * NZ + z for y in range(NY)] for z in range(NZ)]
ROW_GROUPS = [[y * NZ + p + 2 * i for i in range(4)] for y in range(NY) for p in range(2)]
OUT_GROUPS = [[g * 16 + i for i in range(16)] for g in range(NY * NZ // 2)]


def y_shift(d):
    return [(y * NZ + z, ((y + d) % NY) * NZ + z) for y in range(NY) for z in range(NZ)]


def y_later(d):
    return [(y * NZ + z, (y + d) * NZ + z) for y in range(NY - d) for z in range(NZ)]


PAIR = [(s, s ^ 1) for s in range(NY * NZ)]


def after(value, *earlier):
    return lax.optimization_barrier((value,) + earlier)[0]


def whole(count):
    return [pl.BlockSpec(memory_space=VMEM)] * count


def mm(a, b, dims=(((1,), (0,)), ((), ()))):
    return lax.dot_general(a, b, dims, preferred_element_type=F32)


def write_message(ref, head, state, decay):
    ref[head, :E, :] = state.astype(BF16)
    decay = jnp.broadcast_to(decay, (EXTRA, E))
    high = decay.astype(BF16)
    rest = decay - high.astype(F32)
    middle = rest.astype(BF16)
    low = (rest - middle.astype(F32)).astype(BF16)
    row = lax.broadcasted_iota(jnp.int32, (EXTRA, E), 0)
    part = jnp.where(row == 0, high.astype(F32), jnp.where(row == 1, middle.astype(F32), low.astype(F32)))
    ref[head, E:, :] = part.astype(BF16)


def read_decay(ref, head):
    rows = ref[head, E:, :].astype(F32)
    return (rows[0:1] + rows[1:2]) + rows[2:3]


def pieces_kernel(weight_ref, out_ref):
    for c in range(3):
        for i in range(NZ):
            half = slice((i % 2) * 256, (i % 2 + 1) * 256)
            out_ref[i, :, c * 256 : (c + 1) * 256] = weight_ref[c, :, half]


def order_kernel(sent_ref, out_ref):
    for s in range(2):
        for h in range(NH):
            out_ref[:, (h * 2 + s) * 256 : (h * 2 + s + 1) * 256] = sent_ref[s * NH + h]


def states_kernel(total_ref, last_ref, col_ref, row_ref, proj_ref, prefix_ref, message_ref):
    for half in range(2):
        part = slice(half * 512, (half + 1) * 512)
        proj_ref[half] = (total_ref[part] + last_ref[part]).astype(BF16)
    for head in range(2):
        state = jnp.zeros((E, E), F32)
        decay = jnp.zeros((1, 1), F32)
        for n in range(8):
            at = head * 8 + n
            rows = slice((n % 4) * BLK, (n % 4 + 1) * BLK)
            keys = proj_ref[n // 4, rows, head * E : (head + 1) * E]
            values = proj_ref[n // 4, rows, 256 + head * E : 256 + (head + 1) * E]
            last = row_ref[at : at + 1, BLK - 1 : BLK]
            scale = jnp.exp(last - col_ref[:, at : at + 1])
            prefix_ref[at] = state.astype(BF16)
            scaled = (keys.astype(F32) * scale).astype(BF16)
            state = jnp.exp(last) * state + mm(scaled, values, (((0,), (0,)), ((), ())))
            decay = decay + last
        for copy in range(4):
            write_message(message_ref.at[copy], head, state, decay)


def local_kernel(total_ref, proj_ref, prefix_ref, col_ref, row_ref, query_ref, out_ref):
    for half in range(2):
        query_ref[half] = total_ref[half * 512 : (half + 1) * 512].astype(BF16)
    causal = lax.broadcasted_iota(jnp.int32, (BLK, BLK), 0) >= lax.broadcasted_iota(jnp.int32, (BLK, BLK), 1)
    for head in range(2):
        for n in range(8):
            at = head * 8 + n
            rows = slice((n % 4) * BLK, (n % 4 + 1) * BLK)
            queries = query_ref[n // 4, rows, head * E : (head + 1) * E]
            keys = proj_ref[n // 4, rows, head * E : (head + 1) * E]
            values = proj_ref[n // 4, rows, 256 + head * E : 256 + (head + 1) * E]
            col = col_ref[:, at : at + 1]
            gaps = col - row_ref[at : at + 1, :]
            weights = jnp.exp(jnp.where(causal, gaps, -1e30))
            scores = mm(queries, keys, (((1,), (1,)), ((), ()))) * weights
            scaled = (queries.astype(F32) * jnp.exp(col)).astype(BF16)
            out_ref[at] = mm(scores.astype(BF16), values) + mm(scaled, prefix_ref[at])


def row_kernel(place_ref, messages_ref, before_ref, decay_ref, message_ref):
    place = place_ref[0]
    for head in range(2):
        before = jnp.zeros((E, E), F32)
        total = jnp.zeros((E, E), F32)
        gone_before = jnp.zeros((1, E), F32)
        gone = jnp.zeros((1, E), F32)
        for k in (3, 2, 1, 0):
            block = messages_ref[k, head, :E, :].astype(F32)
            decay = read_decay(messages_ref.at[k], head)
            total = total + jnp.exp(gone) * block
            gone = gone + decay
            early = k < place
            before = before + jnp.where(early, jnp.exp(gone_before), 0.0) * block
            gone_before = gone_before + jnp.where(early, decay, 0.0)
        before_ref[head] = before
        decay_ref[head] = jnp.broadcast_to(gone_before, (8, E))
        write_message(message_ref, head, total, gone)


def final_kernel(*refs):
    messages = refs[:7]
    before_ref, decay_ref, part_ref, query_ref, col_ref, start_ref, gain_ref, out_ref = refs[7:]
    for head in range(2):
        carried = jnp.zeros((E, E), F32)
        gone = jnp.zeros((1, E), F32)
        for ref in messages:
            carried = carried + jnp.exp(gone) * ref[head, :E, :].astype(F32)
            gone = gone + read_decay(ref, head)
        incoming = (jnp.exp(decay_ref[head, 0:1, :]) * carried + before_ref[head]).astype(BF16)
        gain = gain_ref[0:1, head * E : (head + 1) * E]
        for n in range(8):
            at = head * 8 + n
            rows = slice((n % 4) * BLK, (n % 4 + 1) * BLK)
            queries = query_ref[n // 4, rows, head * E : (head + 1) * E]
            scale = jnp.exp(col_ref[:, at : at + 1] + start_ref[0:1, at : at + 1])
            scaled = (queries.astype(F32) * scale).astype(BF16)
            output = part_ref[at] + mm(scaled, incoming)
            meansq = jnp.mean(output * output, axis=1, keepdims=True)
            gained = output / jnp.sqrt(meansq + EPS) * gain
            out_ref[n * BLK : (n + 1) * BLK, head * E : (head + 1) * E] = gained.astype(BF16)


def call(kernel, outs, scalars, *args, flops=0):
    shapes = [jax.ShapeDtypeStruct(s, d) for s, d in outs]
    smem = [pl.BlockSpec(memory_space=pltpu.SMEM)] * len(scalars)
    moved = sum(a.size * a.dtype.itemsize for a in args)
    return pl.pallas_call(
        kernel,
        out_shape=shapes,
        in_specs=smem + whole(len(args)),
        out_specs=whole(len(outs)),
        cost_estimate=pl.CostEstimate(flops=flops, bytes_accessed=moved, transcendentals=0),
        compiler_params=pltpu.CompilerParams(vmem_limit_bytes=32 * 1024 * 1024),
    )(*scalars, *args)


def on_device(tokens, qkv_weight, log_decay, norm_gain):
    seq = lax.axis_index("seq")
    y, z = seq // NZ, seq % NZ
    side = z % 2
    place = z // 2
    place1 = place.reshape(1).astype(jnp.int32)

    (pieces,) = call(pieces_kernel, [((NZ, 48, 768), BF16)], [], qkv_weight.transpose(1, 0, 2))
    block = lax.all_to_all(pieces, "seq", split_axis=0, concat_axis=0, tiled=True, axis_index_groups=Z_GROUPS)

    all_rows = lax.all_gather(tokens, ("seq", "head"), axis=0, tiled=True, axis_index_groups=OUT_GROUPS)


    def add(total, part, offset):
        x = lax.dynamic_slice_in_dim(all_rows, ((y + offset) % NY) * (NZ * 48), NZ * 48, 1)
        d = jnp.dot(x, part.reshape(NZ * 48, 512), preferred_element_type=F32)
        return d if total is None else total + d

    query_block = block[:, :, :256]
    block = block[:, :, 256:]
    ups, downs = [block], [block]

    def hop(*earlier):
        ups.append(lax.ppermute(after(ups[-1], *earlier), "seq", y_shift(1)))
        downs.append(lax.ppermute(after(downs[-1], *earlier), "seq", y_shift(-1)))

    def add_step(total, step):
        return add(add(total, ups[step], -step), downs[step], step)

    hop()
    mine = lax.dynamic_slice_in_dim(log_decay, side * 2, 2, 0)
    wanted = lax.dynamic_slice_in_dim(log_decay, (1 - side) * 2, 2, 0)
    theirs = lax.ppermute(after(wanted, block), "seq", PAIR)
    ups.append(lax.ppermute(ups[1], "seq", y_shift(1)))
    downs.append(lax.ppermute(after(downs[1], theirs), "seq", y_shift(-1)))
    both = jnp.where(side == 0, jnp.concatenate([mine, theirs], 1), jnp.concatenate([theirs, mine], 1))
    rows = jnp.cumsum(both.reshape(2, 8, BLK), axis=2)
    ends = rows[:, :, -1]
    starts = (jnp.cumsum(ends, axis=1) - ends).reshape(1, 16)
    rows = rows.reshape(16, BLK)
    cols = rows.T
    gain = lax.dynamic_slice_in_dim(norm_gain, side * 256, 256, 0).reshape(1, 256)

    hop(rows, cols, starts, gain)
    total = add(add(None, block, 0), ups[1], -1)
    query_weight = lax.all_gather(
        after(query_block, all_rows), "seq", axis=0, tiled=True, axis_index_groups=Y_GROUPS
    ).reshape(NY * NZ * 48, 256)
    up4 = lax.ppermute(after(ups[3], total)[:4], "seq", y_shift(1))
    down4 = lax.ppermute(after(downs[3], total)[4:], "seq", y_shift(-1))
    total = add_step(add_step(add(total, downs[1], 1), 2), 3)
    up4, down4, total = lax.optimization_barrier((up4, down4, total))
    last = add(None, jnp.concatenate([up4, down4], 0), 4)

    proj, prefix, messages = call(
        states_kernel,
        [((2, 512, 512), BF16), ((16, E, E), BF16), ((4, 2, E + EXTRA, E), BF16)],
        [], total, last, cols, rows, flops=16 * 2 * E**3,
    )
    messages = lax.all_to_all(messages, "seq", split_axis=0, concat_axis=0, tiled=True, axis_index_groups=ROW_GROUPS)
    query_total = jnp.dot(all_rows, after(query_weight, messages), preferred_element_type=F32)
    query, part = call(
        local_kernel, [((2, 512, 256), BF16), ((16, BLK, E), F32)], [], query_total, proj, prefix, cols, rows,
        flops=16 * 6 * E**3,
    )
    before, gone, row_message = call(
        row_kernel,
        [((2, E, E), F32), ((2, 8, E), F32), ((2, E + EXTRA, E), BF16)],
        [place1], messages,
    )
    earlier = [lax.ppermute(row_message, "seq", y_later(k)) for k in range(1, NY)]
    (flat,) = call(
        final_kernel, [((1024, 256), BF16)], [], *earlier, before, gone, part, query, cols, starts, gain,
        flops=16 * 2 * E**3,
    )
    sent = lax.all_to_all(
        flat.reshape(16, 64, 256), ("seq", "head"), split_axis=0, concat_axis=0, tiled=True,
        axis_index_groups=OUT_GROUPS,
    )
    (out,) = call(order_kernel, [((64, 4096), BF16)], [], sent)
    return out


def solution(mesh):
    return jax.shard_map(
        on_device,
        mesh=mesh,
        in_specs=(P(("seq", "head"), None), P("seq", None, "head"), P("head", "seq"), P("head")),
        out_specs=P(("seq", "head"), None),
        check_vma=False,
    )
```

```python
import functools

import jax
import jax.numpy as jnp
from jax import lax
from jax.experimental import pallas as pl
from jax.experimental.pallas import tpu as pltpu
from jax.sharding import PartitionSpec as P

BLK = 128
E = 128
EPS = 1e-05
NY = 8
NZ = 8
NH = 8
EXTRA = 16
SLICE = 32
F32 = jnp.float32
BF16 = jnp.bfloat16
VMEM = pltpu.VMEM

Z_GROUPS = [[y * NZ + z for z in range(NZ)] for y in range(NY)]
Y_GROUPS = [[y * NZ + z for y in range(NY)] for z in range(NZ)]
ROW_GROUPS = [[y * NZ + p + 2 * i for i in range(4)] for y in range(NY) for p in range(2)]
OUT_GROUPS = [[g * 16 + i for i in range(16)] for g in range(NY * NZ // 2)]


def y_shift(d):
    return [(y * NZ + z, ((y + d) % NY) * NZ + z) for y in range(NY) for z in range(NZ)]


def y_later(d):
    return [(y * NZ + z, (y + d) * NZ + z) for y in range(NY - d) for z in range(NZ)]


PAIR = [(s, s ^ 1) for s in range(NY * NZ)]


def after(value, *earlier):
    return lax.optimization_barrier((value,) + earlier)[0]


def whole(count):
    return [pl.BlockSpec(memory_space=VMEM)] * count


def mm(a, b, dims=(((1,), (0,)), ((), ()))):
    return lax.dot_general(a, b, dims, preferred_element_type=F32)


def write_message(ref, head, state, decay):
    rows = state.shape[0]
    ref[head, :rows, :] = state.astype(BF16)
    decay = jnp.broadcast_to(decay, (EXTRA, E))
    high = decay.astype(BF16)
    rest = decay - high.astype(F32)
    middle = rest.astype(BF16)
    low = (rest - middle.astype(F32)).astype(BF16)
    row = lax.broadcasted_iota(jnp.int32, (EXTRA, E), 0)
    part = jnp.where(row == 0, high.astype(F32), jnp.where(row == 1, middle.astype(F32), low.astype(F32)))
    ref[head, rows:, :] = part.astype(BF16)


def read_decay(ref, head):
    rows = ref[head, SLICE:, :].astype(F32)
    return (rows[0:1] + rows[1:2]) + rows[2:3]


def pieces_kernel(weight_ref, out_ref):
    for c in range(3):
        for i in range(NZ):
            half = slice((i % 2) * 256, (i % 2 + 1) * 256)
            out_ref[i, :, c * 256 : (c + 1) * 256] = weight_ref[c, :, half]


def order_kernel(sent_ref, out_ref):
    for s in range(2):
        for h in range(NH):
            out_ref[:, (h * 2 + s) * 256 : (h * 2 + s + 1) * 256] = sent_ref[s * NH + h]


def states_kernel(total_ref, last_ref, col_ref, row_ref, proj_ref, prefix_ref, message_ref):
    for half in range(2):
        part = slice(half * 512, (half + 1) * 512)
        proj_ref[half] = (total_ref[part] + last_ref[part]).astype(BF16)
    for head in range(2):
        state = jnp.zeros((E, E), F32)
        decay = jnp.zeros((1, 1), F32)
        for n in range(8):
            at = head * 8 + n
            rows = slice((n % 4) * BLK, (n % 4 + 1) * BLK)
            keys = proj_ref[n // 4, rows, head * E : (head + 1) * E]
            values = proj_ref[n // 4, rows, 256 + head * E : 256 + (head + 1) * E]
            last = row_ref[at : at + 1, BLK - 1 : BLK]
            scale = jnp.exp(last - col_ref[:, at : at + 1])
            prefix_ref[at] = state.astype(BF16)
            scaled = (keys.astype(F32) * scale).astype(BF16)
            state = jnp.exp(last) * state + mm(scaled, values, (((0,), (0,)), ((), ())))
            decay = decay + last
        for q in range(4):
            write_message(message_ref.at[q], head, state[q * SLICE : (q + 1) * SLICE], decay)


def local_kernel(total_ref, proj_ref, prefix_ref, col_ref, row_ref, query_ref, out_ref):
    for half in range(2):
        query_ref[half] = total_ref[half * 512 : (half + 1) * 512].astype(BF16)
    causal = lax.broadcasted_iota(jnp.int32, (BLK, BLK), 0) >= lax.broadcasted_iota(jnp.int32, (BLK, BLK), 1)
    for head in range(2):
        for n in range(8):
            at = head * 8 + n
            rows = slice((n % 4) * BLK, (n % 4 + 1) * BLK)
            queries = query_ref[n // 4, rows, head * E : (head + 1) * E]
            keys = proj_ref[n // 4, rows, head * E : (head + 1) * E]
            values = proj_ref[n // 4, rows, 256 + head * E : 256 + (head + 1) * E]
            col = col_ref[:, at : at + 1]
            gaps = col - row_ref[at : at + 1, :]
            weights = jnp.exp(jnp.where(causal, gaps, -1e30))
            scores = mm(queries, keys, (((1,), (1,)), ((), ()))) * weights
            scaled = (queries.astype(F32) * jnp.exp(col)).astype(BF16)
            out_ref[at] = mm(scores.astype(BF16), values) + mm(scaled, prefix_ref[at])


def row_kernel(messages_ref, before_ref, decay_ref, message_ref):
    for head in range(2):
        before = jnp.zeros((SLICE, E), F32)
        gone = jnp.zeros((1, E), F32)
        for k in range(4):
            before_ref[k, head] = before
            decay_ref[k, head] = jnp.broadcast_to(gone, (8, E))
            decay = read_decay(messages_ref.at[k], head)
            before = jnp.exp(decay) * before + messages_ref[k, head, :SLICE, :].astype(F32)
            gone = gone + decay
        write_message(message_ref, head, before, gone)


def column_kernel(*refs):
    messages = refs[:7]
    before_ref, decay_ref, incoming_ref = refs[7:]
    for head in range(2):
        carried = jnp.zeros((SLICE, E), F32)
        gone = jnp.zeros((1, E), F32)
        for ref in messages:
            carried = carried + jnp.exp(gone) * ref[head, :SLICE, :].astype(F32)
            gone = gone + read_decay(ref, head)
        for k in range(4):
            incoming = jnp.exp(decay_ref[k, head, 0:1, :]) * carried + before_ref[k, head]
            incoming_ref[k, head] = incoming.astype(BF16)


def final_kernel(incoming_ref, part_ref, query_ref, col_ref, start_ref, gain_ref, out_ref):
    for head in range(2):
        incoming = incoming_ref[:, head].reshape(E, E)
        gain = gain_ref[0:1, head * E : (head + 1) * E]
        for n in range(8):
            at = head * 8 + n
            rows = slice((n % 4) * BLK, (n % 4 + 1) * BLK)
            queries = query_ref[n // 4, rows, head * E : (head + 1) * E]
            scale = jnp.exp(col_ref[:, at : at + 1] + start_ref[0:1, at : at + 1])
            scaled = (queries.astype(F32) * scale).astype(BF16)
            output = part_ref[at] + mm(scaled, incoming)
            meansq = jnp.mean(output * output, axis=1, keepdims=True)
            gained = output / jnp.sqrt(meansq + EPS) * gain
            out_ref[n * BLK : (n + 1) * BLK, head * E : (head + 1) * E] = gained.astype(BF16)


def call(kernel, outs, scalars, *args, flops=0):
    shapes = [jax.ShapeDtypeStruct(s, d) for s, d in outs]
    smem = [pl.BlockSpec(memory_space=pltpu.SMEM)] * len(scalars)
    moved = sum(a.size * a.dtype.itemsize for a in args)
    return pl.pallas_call(
        kernel,
        out_shape=shapes,
        in_specs=smem + whole(len(args)),
        out_specs=whole(len(outs)),
        cost_estimate=pl.CostEstimate(flops=flops, bytes_accessed=moved, transcendentals=0),
        compiler_params=pltpu.CompilerParams(vmem_limit_bytes=32 * 1024 * 1024),
    )(*scalars, *args)


def on_device(tokens, qkv_weight, log_decay, norm_gain):
    seq = lax.axis_index("seq")
    y, z = seq // NZ, seq % NZ
    side = z % 2

    (pieces,) = call(pieces_kernel, [((NZ, 48, 768), BF16)], [], qkv_weight.transpose(1, 0, 2))
    block = lax.all_to_all(pieces, "seq", split_axis=0, concat_axis=0, tiled=True, axis_index_groups=Z_GROUPS)

    all_rows = lax.all_gather(tokens, ("seq", "head"), axis=0, tiled=True, axis_index_groups=OUT_GROUPS)


    def add(total, part, offset):
        x = lax.dynamic_slice_in_dim(all_rows, ((y + offset) % NY) * (NZ * 48), NZ * 48, 1)
        d = jnp.dot(x, part.reshape(NZ * 48, 512), preferred_element_type=F32)
        return d if total is None else total + d

    query_block = block[:, :, :256]
    block = block[:, :, 256:]
    ups, downs = [block], [block]

    def hop(*earlier):
        ups.append(lax.ppermute(after(ups[-1], *earlier), "seq", y_shift(1)))
        downs.append(lax.ppermute(after(downs[-1], *earlier), "seq", y_shift(-1)))

    def add_step(total, step):
        return add(add(total, ups[step], -step), downs[step], step)

    hop()
    mine = lax.dynamic_slice_in_dim(log_decay, side * 2, 2, 0)
    wanted = lax.dynamic_slice_in_dim(log_decay, (1 - side) * 2, 2, 0)
    theirs = lax.ppermute(after(wanted, block), "seq", PAIR)
    ups.append(lax.ppermute(ups[1], "seq", y_shift(1)))
    downs.append(lax.ppermute(after(downs[1], theirs), "seq", y_shift(-1)))
    both = jnp.where(side == 0, jnp.concatenate([mine, theirs], 1), jnp.concatenate([theirs, mine], 1))
    rows = jnp.cumsum(both.reshape(2, 8, BLK), axis=2)
    ends = rows[:, :, -1]
    starts = (jnp.cumsum(ends, axis=1) - ends).reshape(1, 16)
    rows = rows.reshape(16, BLK)
    cols = rows.T
    gain = lax.dynamic_slice_in_dim(norm_gain, side * 256, 256, 0).reshape(1, 256)

    hop(rows, cols, starts, gain)
    total = add(add(None, block, 0), ups[1], -1)
    query_weight = lax.all_gather(
        after(query_block, all_rows), "seq", axis=0, tiled=True, axis_index_groups=Y_GROUPS
    ).reshape(NY * NZ * 48, 256)
    up4 = lax.ppermute(after(ups[3], total)[:4], "seq", y_shift(1))
    down4 = lax.ppermute(after(downs[3], total)[4:], "seq", y_shift(-1))
    total = add_step(add_step(add(total, downs[1], 1), 2), 3)
    up4, down4, total = lax.optimization_barrier((up4, down4, total))
    last = add(None, jnp.concatenate([up4, down4], 0), 4)

    proj, prefix, messages = call(
        states_kernel,
        [((2, 512, 512), BF16), ((16, E, E), BF16), ((4, 2, SLICE + EXTRA, E), BF16)],
        [], total, last, cols, rows, flops=16 * 2 * E**3,
    )
    messages = lax.all_to_all(messages, "seq", split_axis=0, concat_axis=0, tiled=True, axis_index_groups=ROW_GROUPS)
    query_total = jnp.dot(all_rows, after(query_weight, messages), preferred_element_type=F32)
    query, part = call(
        local_kernel, [((2, 512, 256), BF16), ((16, BLK, E), F32)], [], query_total, proj, prefix, cols, rows,
        flops=16 * 6 * E**3,
    )
    before, gone, row_message = call(
        row_kernel,
        [((4, 2, SLICE, E), F32), ((4, 2, 8, E), F32), ((2, SLICE + EXTRA, E), BF16)],
        [], messages,
    )
    earlier = [lax.ppermute(row_message, "seq", y_later(k)) for k in range(1, NY)]
    (incoming,) = call(column_kernel, [((4, 2, SLICE, E), BF16)], [], *earlier, after(before, query_total), gone)
    incoming = lax.all_to_all(
        incoming, "seq", split_axis=0, concat_axis=0, tiled=True, axis_index_groups=ROW_GROUPS
    )
    (flat,) = call(
        final_kernel, [((1024, 256), BF16)], [], incoming, part, query, cols, starts, gain,
        flops=16 * 2 * E**3,
    )
    sent = lax.all_to_all(
        flat.reshape(16, 64, 256), ("seq", "head"), split_axis=0, concat_axis=0, tiled=True,
        axis_index_groups=OUT_GROUPS,
    )
    (out,) = call(order_kernel, [((64, 4096), BF16)], [], sent)
    return out


def solution(mesh):
    return jax.shard_map(
        on_device,
        mesh=mesh,
        in_specs=(P(("seq", "head"), None), P("seq", None, "head"), P("head", "seq"), P("head")),
        out_specs=P(("seq", "head"), None),
        check_vma=False,
    )
```

```python
import functools

import jax
import jax.numpy as jnp
from jax import lax
from jax.experimental import pallas as pl
from jax.experimental.pallas import tpu as pltpu
from jax.sharding import PartitionSpec as P

BLK = 128
E = 128
EPS = 1e-05
NY = 8
NZ = 8
NH = 8
EXTRA = 16
FAR_FIRST = (4, 3, 5, 2, 6, 1, 7)
F32 = jnp.float32
BF16 = jnp.bfloat16
VMEM = pltpu.VMEM

Z_GROUPS = [[y * NZ + z for z in range(NZ)] for y in range(NY)]
Y_GROUPS = [[y * NZ + z for y in range(NY)] for z in range(NZ)]
ROW_GROUPS = [[y * NZ + p + 2 * i for i in range(4)] for y in range(NY) for p in range(2)]
OUT_GROUPS = [[g * 16 + i for i in range(16)] for g in range(NY * NZ // 2)]


def y_shift(d):
    return [(y * NZ + z, ((y + d) % NY) * NZ + z) for y in range(NY) for z in range(NZ)]


def y_later(d):
    return [(y * NZ + z, (y + d) * NZ + z) for y in range(NY - d) for z in range(NZ)]


PAIR = [(s, s ^ 1) for s in range(NY * NZ)]


def after(value, *earlier):
    return lax.optimization_barrier((value,) + earlier)[0]


def whole(count):
    return [pl.BlockSpec(memory_space=VMEM)] * count


def mm(a, b, dims=(((1,), (0,)), ((), ()))):
    return lax.dot_general(a, b, dims, preferred_element_type=F32)


def write_message(refs, head, state, decay):
    decay = jnp.broadcast_to(decay, (EXTRA, E))
    high = decay.astype(BF16)
    rest = decay - high.astype(F32)
    middle = rest.astype(BF16)
    low = (rest - middle.astype(F32)).astype(BF16)
    row = lax.broadcasted_iota(jnp.int32, (EXTRA, E), 0)
    part = jnp.where(row == 0, high.astype(F32), jnp.where(row == 1, middle.astype(F32), low.astype(F32)))
    part = part.astype(BF16)
    state = state.astype(BF16)
    for ref in refs:
        ref[head, :E, :] = state
        ref[head, E:, :] = part


def read_decay(ref, head):
    rows = ref[head, E:, :].astype(F32)
    return (rows[0:1] + rows[1:2]) + rows[2:3]


def pieces_kernel(weight_ref, out_ref):
    for c in range(3):
        for i in range(NZ):
            half = slice((i % 2) * 256, (i % 2 + 1) * 256)
            out_ref[i, :, c * 256 : (c + 1) * 256] = weight_ref[c, :, half]


def order_kernel(sent_ref, out_ref):
    for s in range(2):
        for h in range(NH):
            out_ref[:, (h * 2 + s) * 256 : (h * 2 + s + 1) * 256] = sent_ref[s * NH + h]


def states_kernel(total_ref, last_ref, col_ref, row_ref, proj_ref, prefix_ref, message_ref):
    for half in range(2):
        part = slice(half * 512, (half + 1) * 512)
        proj_ref[half] = (total_ref[part] + last_ref[part]).astype(BF16)
    for head in range(2):
        state = jnp.zeros((E, E), F32)
        decay = jnp.zeros((1, 1), F32)
        for n in range(8):
            at = head * 8 + n
            rows = slice((n % 4) * BLK, (n % 4 + 1) * BLK)
            keys = proj_ref[n // 4, rows, head * E : (head + 1) * E]
            values = proj_ref[n // 4, rows, 256 + head * E : 256 + (head + 1) * E]
            last = row_ref[at : at + 1, BLK - 1 : BLK]
            scale = jnp.exp(last - col_ref[:, at : at + 1])
            prefix_ref[at] = state.astype(BF16)
            scaled = (keys.astype(F32) * scale).astype(BF16)
            state = jnp.exp(last) * state + mm(scaled, values, (((0,), (0,)), ((), ())))
            decay = decay + last
        write_message([message_ref.at[k] for k in range(4)], head, state, decay)


def local_kernel(total_ref, proj_ref, prefix_ref, col_ref, row_ref, query_ref, out_ref):
    for half in range(2):
        query_ref[half] = total_ref[half * 512 : (half + 1) * 512].astype(BF16)
    causal = lax.broadcasted_iota(jnp.int32, (BLK, BLK), 0) >= lax.broadcasted_iota(jnp.int32, (BLK, BLK), 1)
    for head in range(2):
        for n in range(8):
            at = head * 8 + n
            rows = slice((n % 4) * BLK, (n % 4 + 1) * BLK)
            queries = query_ref[n // 4, rows, head * E : (head + 1) * E]
            keys = proj_ref[n // 4, rows, head * E : (head + 1) * E]
            values = proj_ref[n // 4, rows, 256 + head * E : 256 + (head + 1) * E]
            col = col_ref[:, at : at + 1]
            gaps = col - row_ref[at : at + 1, :]
            weights = jnp.exp(jnp.where(causal, gaps, -1e30))
            scores = mm(queries, keys, (((1,), (1,)), ((), ()))) * weights
            scaled = (queries.astype(F32) * jnp.exp(col)).astype(BF16)
            out_ref[at] = mm(scores.astype(BF16), values) + mm(scaled, prefix_ref[at])


def row_kernel(place_ref, messages_ref, before_ref, decay_ref, message_ref):
    place = place_ref[0]
    for head in range(2):
        before = jnp.zeros((E, E), F32)
        total = jnp.zeros((E, E), F32)
        gone_before = jnp.zeros((1, E), F32)
        gone = jnp.zeros((1, E), F32)
        for k in (3, 2, 1, 0):
            block = messages_ref[k, head, :E, :].astype(F32)
            decay = read_decay(messages_ref.at[k], head)
            total = total + jnp.exp(gone) * block
            gone = gone + decay
            early = k < place
            before = before + jnp.where(early, jnp.exp(gone_before), 0.0) * block
            gone_before = gone_before + jnp.where(early, decay, 0.0)
        before_ref[head] = before
        decay_ref[head] = jnp.broadcast_to(gone_before, (8, E))
        write_message([message_ref], head, total, gone)


def final_kernel(*refs):
    messages = [refs[FAR_FIRST.index(k)] for k in range(1, NY)]
    before_ref, decay_ref, part_ref, query_ref, col_ref, start_ref, gain_ref, out_ref = refs[7:]
    for head in range(2):
        carried = jnp.zeros((E, E), F32)
        gone = jnp.zeros((1, E), F32)
        for ref in messages:
            carried = carried + jnp.exp(gone) * ref[head, :E, :].astype(F32)
            gone = gone + read_decay(ref, head)
        incoming = (jnp.exp(decay_ref[head, 0:1, :]) * carried + before_ref[head]).astype(BF16)
        gain = gain_ref[0:1, head * E : (head + 1) * E]
        for n in range(8):
            at = head * 8 + n
            rows = slice((n % 4) * BLK, (n % 4 + 1) * BLK)
            queries = query_ref[n // 4, rows, head * E : (head + 1) * E]
            scale = jnp.exp(col_ref[:, at : at + 1] + start_ref[0:1, at : at + 1])
            scaled = (queries.astype(F32) * scale).astype(BF16)
            output = part_ref[at] + mm(scaled, incoming)
            meansq = jnp.mean(output * output, axis=1, keepdims=True)
            gained = output / jnp.sqrt(meansq + EPS) * gain
            out_ref[n * BLK : (n + 1) * BLK, head * E : (head + 1) * E] = gained.astype(BF16)


def call(kernel, outs, scalars, *args, flops=0):
    shapes = [jax.ShapeDtypeStruct(s, d) for s, d in outs]
    smem = [pl.BlockSpec(memory_space=pltpu.SMEM)] * len(scalars)
    moved = sum(a.size * a.dtype.itemsize for a in args)
    return pl.pallas_call(
        kernel,
        out_shape=shapes,
        in_specs=smem + whole(len(args)),
        out_specs=whole(len(outs)),
        cost_estimate=pl.CostEstimate(flops=flops, bytes_accessed=moved, transcendentals=0),
        compiler_params=pltpu.CompilerParams(vmem_limit_bytes=32 * 1024 * 1024),
    )(*scalars, *args)


def on_device(tokens, qkv_weight, log_decay, norm_gain):
    seq = lax.axis_index("seq")
    y, z = seq // NZ, seq % NZ
    side = z % 2
    place = z // 2
    place1 = place.reshape(1).astype(jnp.int32)

    (pieces,) = call(pieces_kernel, [((NZ, 48, 768), BF16)], [], qkv_weight.transpose(1, 0, 2))
    block = lax.all_to_all(pieces, "seq", split_axis=0, concat_axis=0, tiled=True, axis_index_groups=Z_GROUPS)

    all_rows = lax.all_gather(tokens, ("seq", "head"), axis=0, tiled=True, axis_index_groups=OUT_GROUPS)


    def add(total, part, offset):
        x = lax.dynamic_slice_in_dim(all_rows, ((y + offset) % NY) * (NZ * 48), NZ * 48, 1)
        d = jnp.dot(x, part.reshape(NZ * 48, 512), preferred_element_type=F32)
        return d if total is None else total + d

    query_block = block[:, :, :256]
    block = block[:, :, 256:]
    ups, downs = [block], [block]

    def hop(*earlier):
        ups.append(lax.ppermute(after(ups[-1], *earlier), "seq", y_shift(1)))
        downs.append(lax.ppermute(after(downs[-1], *earlier), "seq", y_shift(-1)))

    def add_step(total, step):
        return add(add(total, ups[step], -step), downs[step], step)

    hop()
    mine = lax.dynamic_slice_in_dim(log_decay, side * 2, 2, 0)
    wanted = lax.dynamic_slice_in_dim(log_decay, (1 - side) * 2, 2, 0)
    theirs = lax.ppermute(after(wanted, block), "seq", PAIR)
    ups.append(lax.ppermute(ups[1], "seq", y_shift(1)))
    downs.append(lax.ppermute(after(downs[1], theirs), "seq", y_shift(-1)))
    both = jnp.where(side == 0, jnp.concatenate([mine, theirs], 1), jnp.concatenate([theirs, mine], 1))
    rows = jnp.cumsum(both.reshape(2, 8, BLK), axis=2)
    ends = rows[:, :, -1]
    starts = (jnp.cumsum(ends, axis=1) - ends).reshape(1, 16)
    rows = rows.reshape(16, BLK)
    cols = rows.T
    gain = lax.dynamic_slice_in_dim(norm_gain, side * 256, 256, 0).reshape(1, 256)

    hop(rows, cols, starts, gain)
    total = add(add(None, block, 0), ups[1], -1)
    query_weight = lax.all_gather(
        after(query_block, all_rows), "seq", axis=0, tiled=True, axis_index_groups=Y_GROUPS
    ).reshape(NY * NZ * 48, 256)
    up4 = lax.ppermute(after(ups[3], total)[:4], "seq", y_shift(1))
    down4 = lax.ppermute(after(downs[3], total)[4:], "seq", y_shift(-1))
    total = add_step(add_step(add(total, downs[1], 1), 2), 3)
    up4, down4, total = lax.optimization_barrier((up4, down4, total))
    last = add(None, jnp.concatenate([up4, down4], 0), 4)

    proj, prefix, messages = call(
        states_kernel,
        [((2, 512, 512), BF16), ((16, E, E), BF16), ((4, 2, E + EXTRA, E), BF16)],
        [], total, last, cols, rows, flops=16 * 2 * E**3,
    )
    messages = lax.all_to_all(messages, "seq", split_axis=0, concat_axis=0, tiled=True, axis_index_groups=ROW_GROUPS)
    query_total = jnp.dot(all_rows, after(query_weight, messages), preferred_element_type=F32)
    query, part = call(
        local_kernel, [((2, 512, 256), BF16), ((16, BLK, E), F32)], [], query_total, proj, prefix, cols, rows,
        flops=16 * 6 * E**3,
    )
    before, gone, row_message = call(
        row_kernel,
        [((2, E, E), F32), ((2, 8, E), F32), ((2, E + EXTRA, E), BF16)],
        [place1], messages,
    )
    earlier = [lax.ppermute(row_message, "seq", y_later(k)) for k in FAR_FIRST]
    (flat,) = call(
        final_kernel, [((1024, 256), BF16)], [], *earlier, before, gone, part, query, cols, starts, gain,
        flops=16 * 2 * E**3,
    )
    sent = lax.all_to_all(
        flat.reshape(16, 64, 256), ("seq", "head"), split_axis=0, concat_axis=0, tiled=True,
        axis_index_groups=OUT_GROUPS,
    )
    (out,) = call(order_kernel, [((64, 4096), BF16)], [], sent)
    return out


def solution(mesh):
    return jax.shard_map(
        on_device,
        mesh=mesh,
        in_specs=(P(("seq", "head"), None), P("seq", None, "head"), P("head", "seq"), P("head")),
        out_specs=P(("seq", "head"), None),
        check_vma=False,
    )
```

```python
import functools

import jax
import jax.numpy as jnp
from jax import lax
from jax.experimental import pallas as pl
from jax.experimental.pallas import tpu as pltpu
from jax.sharding import PartitionSpec as P

BLK = 128
E = 128
EPS = 1e-05
NY = 8
NZ = 8
NH = 8
EXTRA = 16
START_ORDER = (1, 7, 4, 3, 5, 2, 6)
F32 = jnp.float32
BF16 = jnp.bfloat16
VMEM = pltpu.VMEM

Z_GROUPS = [[y * NZ + z for z in range(NZ)] for y in range(NY)]
Y_GROUPS = [[y * NZ + z for y in range(NY)] for z in range(NZ)]
ROW_GROUPS = [[y * NZ + p + 2 * i for i in range(4)] for y in range(NY) for p in range(2)]
OUT_GROUPS = [[g * 16 + i for i in range(16)] for g in range(NY * NZ // 2)]


def y_shift(d):
    return [(y * NZ + z, ((y + d) % NY) * NZ + z) for y in range(NY) for z in range(NZ)]


def y_later(d):
    return [(y * NZ + z, (y + d) * NZ + z) for y in range(NY - d) for z in range(NZ)]


PAIR = [(s, s ^ 1) for s in range(NY * NZ)]


def after(value, *earlier):
    return lax.optimization_barrier((value,) + earlier)[0]


def whole(count):
    return [pl.BlockSpec(memory_space=VMEM)] * count


def mm(a, b, dims=(((1,), (0,)), ((), ()))):
    return lax.dot_general(a, b, dims, preferred_element_type=F32)


def write_message(refs, head, state, decay):
    decay = jnp.broadcast_to(decay, (EXTRA, E))
    high = decay.astype(BF16)
    rest = decay - high.astype(F32)
    middle = rest.astype(BF16)
    low = (rest - middle.astype(F32)).astype(BF16)
    row = lax.broadcasted_iota(jnp.int32, (EXTRA, E), 0)
    part = jnp.where(row == 0, high.astype(F32), jnp.where(row == 1, middle.astype(F32), low.astype(F32)))
    part = part.astype(BF16)
    state = state.astype(BF16)
    for ref in refs:
        ref[head, :E, :] = state
        ref[head, E:, :] = part


def read_decay(ref, head):
    rows = ref[head, E:, :].astype(F32)
    return (rows[0:1] + rows[1:2]) + rows[2:3]


def pieces_kernel(weight_ref, out_ref):
    for c in range(3):
        for i in range(NZ):
            half = slice((i % 2) * 256, (i % 2 + 1) * 256)
            out_ref[i, :, c * 256 : (c + 1) * 256] = weight_ref[c, :, half]


def order_kernel(sent_ref, out_ref):
    for s in range(2):
        for h in range(NH):
            out_ref[:, (h * 2 + s) * 256 : (h * 2 + s + 1) * 256] = sent_ref[s * NH + h]


def states_kernel(total_ref, last_ref, col_ref, row_ref, proj_ref, prefix_ref, message_ref):
    for half in range(2):
        part = slice(half * 512, (half + 1) * 512)
        proj_ref[half] = (total_ref[part] + last_ref[part]).astype(BF16)
    for head in range(2):
        state = jnp.zeros((E, E), F32)
        decay = jnp.zeros((1, 1), F32)
        for n in range(8):
            at = head * 8 + n
            rows = slice((n % 4) * BLK, (n % 4 + 1) * BLK)
            keys = proj_ref[n // 4, rows, head * E : (head + 1) * E]
            values = proj_ref[n // 4, rows, 256 + head * E : 256 + (head + 1) * E]
            last = row_ref[at : at + 1, BLK - 1 : BLK]
            scale = jnp.exp(last - col_ref[:, at : at + 1])
            prefix_ref[at] = state.astype(BF16)
            scaled = (keys.astype(F32) * scale).astype(BF16)
            state = jnp.exp(last) * state + mm(scaled, values, (((0,), (0,)), ((), ())))
            decay = decay + last
        write_message([message_ref.at[k] for k in range(4)], head, state, decay)


def local_kernel(total_ref, proj_ref, prefix_ref, col_ref, row_ref, query_ref, out_ref):
    for half in range(2):
        query_ref[half] = total_ref[half * 512 : (half + 1) * 512].astype(BF16)
    causal = lax.broadcasted_iota(jnp.int32, (BLK, BLK), 0) >= lax.broadcasted_iota(jnp.int32, (BLK, BLK), 1)
    for head in range(2):
        for n in range(8):
            at = head * 8 + n
            rows = slice((n % 4) * BLK, (n % 4 + 1) * BLK)
            queries = query_ref[n // 4, rows, head * E : (head + 1) * E]
            keys = proj_ref[n // 4, rows, head * E : (head + 1) * E]
            values = proj_ref[n // 4, rows, 256 + head * E : 256 + (head + 1) * E]
            col = col_ref[:, at : at + 1]
            gaps = col - row_ref[at : at + 1, :]
            weights = jnp.exp(jnp.where(causal, gaps, -1e30))
            scores = mm(queries, keys, (((1,), (1,)), ((), ()))) * weights
            scaled = (queries.astype(F32) * jnp.exp(col)).astype(BF16)
            out_ref[at] = mm(scores.astype(BF16), values) + mm(scaled, prefix_ref[at])


def row_kernel(place_ref, messages_ref, before_ref, decay_ref, message_ref):
    place = place_ref[0]
    for head in range(2):
        before = jnp.zeros((E, E), F32)
        total = jnp.zeros((E, E), F32)
        gone_before = jnp.zeros((1, E), F32)
        gone = jnp.zeros((1, E), F32)
        for k in (3, 2, 1, 0):
            block = messages_ref[k, head, :E, :].astype(F32)
            decay = read_decay(messages_ref.at[k], head)
            total = total + jnp.exp(gone) * block
            gone = gone + decay
            early = k < place
            before = before + jnp.where(early, jnp.exp(gone_before), 0.0) * block
            gone_before = gone_before + jnp.where(early, decay, 0.0)
        before_ref[head] = before
        decay_ref[head] = jnp.broadcast_to(gone_before, (8, E))
        write_message([message_ref], head, total, gone)


def final_kernel(*refs):
    messages = [refs[START_ORDER.index(k)] for k in range(1, NY)]
    before_ref, decay_ref, part_ref, query_ref, col_ref, start_ref, gain_ref, out_ref = refs[7:]
    for head in range(2):
        carried = jnp.zeros((E, E), F32)
        gone = jnp.zeros((1, E), F32)
        for ref in messages:
            carried = carried + jnp.exp(gone) * ref[head, :E, :].astype(F32)
            gone = gone + read_decay(ref, head)
        incoming = (jnp.exp(decay_ref[head, 0:1, :]) * carried + before_ref[head]).astype(BF16)
        gain = gain_ref[0:1, head * E : (head + 1) * E]
        for n in range(8):
            at = head * 8 + n
            rows = slice((n % 4) * BLK, (n % 4 + 1) * BLK)
            queries = query_ref[n // 4, rows, head * E : (head + 1) * E]
            scale = jnp.exp(col_ref[:, at : at + 1] + start_ref[0:1, at : at + 1])
            scaled = (queries.astype(F32) * scale).astype(BF16)
            output = part_ref[at] + mm(scaled, incoming)
            meansq = jnp.mean(output * output, axis=1, keepdims=True)
            gained = output / jnp.sqrt(meansq + EPS) * gain
            out_ref[n * BLK : (n + 1) * BLK, head * E : (head + 1) * E] = gained.astype(BF16)


def call(kernel, outs, scalars, *args, flops=0):
    shapes = [jax.ShapeDtypeStruct(s, d) for s, d in outs]
    smem = [pl.BlockSpec(memory_space=pltpu.SMEM)] * len(scalars)
    moved = sum(a.size * a.dtype.itemsize for a in args)
    return pl.pallas_call(
        kernel,
        out_shape=shapes,
        in_specs=smem + whole(len(args)),
        out_specs=whole(len(outs)),
        cost_estimate=pl.CostEstimate(flops=flops, bytes_accessed=moved, transcendentals=0),
        compiler_params=pltpu.CompilerParams(vmem_limit_bytes=32 * 1024 * 1024),
    )(*scalars, *args)


def on_device(tokens, qkv_weight, log_decay, norm_gain):
    seq = lax.axis_index("seq")
    y, z = seq // NZ, seq % NZ
    side = z % 2
    place = z // 2
    place1 = place.reshape(1).astype(jnp.int32)

    (pieces,) = call(pieces_kernel, [((NZ, 48, 768), BF16)], [], qkv_weight.transpose(1, 0, 2))
    block = lax.all_to_all(pieces, "seq", split_axis=0, concat_axis=0, tiled=True, axis_index_groups=Z_GROUPS)

    all_rows = lax.all_gather(tokens, ("seq", "head"), axis=0, tiled=True, axis_index_groups=OUT_GROUPS)


    def add(total, part, offset):
        x = lax.dynamic_slice_in_dim(all_rows, ((y + offset) % NY) * (NZ * 48), NZ * 48, 1)
        d = jnp.dot(x, part.reshape(NZ * 48, 512), preferred_element_type=F32)
        return d if total is None else total + d

    query_block = block[:, :, :256]
    block = block[:, :, 256:]
    ups, downs = [block], [block]

    def hop(*earlier):
        ups.append(lax.ppermute(after(ups[-1], *earlier), "seq", y_shift(1)))
        downs.append(lax.ppermute(after(downs[-1], *earlier), "seq", y_shift(-1)))

    def add_step(total, step):
        return add(add(total, ups[step], -step), downs[step], step)

    hop()
    mine = lax.dynamic_slice_in_dim(log_decay, side * 2, 2, 0)
    wanted = lax.dynamic_slice_in_dim(log_decay, (1 - side) * 2, 2, 0)
    theirs = lax.ppermute(after(wanted, block), "seq", PAIR)
    ups.append(lax.ppermute(ups[1], "seq", y_shift(1)))
    downs.append(lax.ppermute(after(downs[1], theirs), "seq", y_shift(-1)))
    both = jnp.where(side == 0, jnp.concatenate([mine, theirs], 1), jnp.concatenate([theirs, mine], 1))
    rows = jnp.cumsum(both.reshape(2, 8, BLK), axis=2)
    ends = rows[:, :, -1]
    starts = (jnp.cumsum(ends, axis=1) - ends).reshape(1, 16)
    rows = rows.reshape(16, BLK)
    cols = rows.T
    gain = lax.dynamic_slice_in_dim(norm_gain, side * 256, 256, 0).reshape(1, 256)

    hop(rows, cols, starts, gain)
    total = add(add(None, block, 0), ups[1], -1)
    query_weight = lax.all_gather(
        after(query_block, all_rows), "seq", axis=0, tiled=True, axis_index_groups=Y_GROUPS
    ).reshape(NY * NZ * 48, 256)
    up4 = lax.ppermute(after(ups[3], total)[:4], "seq", y_shift(1))
    down4 = lax.ppermute(after(downs[3], total)[4:], "seq", y_shift(-1))
    total = add_step(add_step(add(total, downs[1], 1), 2), 3)
    up4, down4, total = lax.optimization_barrier((up4, down4, total))
    last = add(None, jnp.concatenate([up4, down4], 0), 4)

    proj, prefix, messages = call(
        states_kernel,
        [((2, 512, 512), BF16), ((16, E, E), BF16), ((4, 2, E + EXTRA, E), BF16)],
        [], total, last, cols, rows, flops=16 * 2 * E**3,
    )
    messages = lax.all_to_all(messages, "seq", split_axis=0, concat_axis=0, tiled=True, axis_index_groups=ROW_GROUPS)
    query_total = jnp.dot(all_rows, after(query_weight, messages), preferred_element_type=F32)
    query, part = call(
        local_kernel, [((2, 512, 256), BF16), ((16, BLK, E), F32)], [], query_total, proj, prefix, cols, rows,
        flops=16 * 6 * E**3,
    )
    before, gone, row_message = call(
        row_kernel,
        [((2, E, E), F32), ((2, 8, E), F32), ((2, E + EXTRA, E), BF16)],
        [place1], messages,
    )
    earlier = [lax.ppermute(row_message, "seq", y_later(k)) for k in START_ORDER]
    (flat,) = call(
        final_kernel, [((1024, 256), BF16)], [], *earlier, before, gone, part, query, cols, starts, gain,
        flops=16 * 2 * E**3,
    )
    sent = lax.all_to_all(
        flat.reshape(16, 64, 256), ("seq", "head"), split_axis=0, concat_axis=0, tiled=True,
        axis_index_groups=OUT_GROUPS,
    )
    (out,) = call(order_kernel, [((64, 4096), BF16)], [], sent)
    return out


def solution(mesh):
    return jax.shard_map(
        on_device,
        mesh=mesh,
        in_specs=(P(("seq", "head"), None), P("seq", None, "head"), P("head", "seq"), P("head")),
        out_specs=P(("seq", "head"), None),
        check_vma=False,
    )
```

```python
import functools

import jax
import jax.numpy as jnp
from jax import lax
from jax.experimental import pallas as pl
from jax.experimental.pallas import tpu as pltpu
from jax.sharding import PartitionSpec as P

BLK = 128
E = 128
EPS = 1e-05
NY = 8
NZ = 8
NH = 8
EXTRA = 16
START_ORDER = (1, 2, 4, 5, 3, 6, 7)
F32 = jnp.float32
BF16 = jnp.bfloat16
VMEM = pltpu.VMEM

Z_GROUPS = [[y * NZ + z for z in range(NZ)] for y in range(NY)]
Y_GROUPS = [[y * NZ + z for y in range(NY)] for z in range(NZ)]
ROW_GROUPS = [[y * NZ + p + 2 * i for i in range(4)] for y in range(NY) for p in range(2)]
OUT_GROUPS = [[g * 16 + i for i in range(16)] for g in range(NY * NZ // 2)]


def y_shift(d):
    return [(y * NZ + z, ((y + d) % NY) * NZ + z) for y in range(NY) for z in range(NZ)]


def y_later(d):
    return [(y * NZ + z, (y + d) * NZ + z) for y in range(NY - d) for z in range(NZ)]


PAIR = [(s, s ^ 1) for s in range(NY * NZ)]


def after(value, *earlier):
    return lax.optimization_barrier((value,) + earlier)[0]


def whole(count):
    return [pl.BlockSpec(memory_space=VMEM)] * count


def mm(a, b, dims=(((1,), (0,)), ((), ()))):
    return lax.dot_general(a, b, dims, preferred_element_type=F32)


def write_message(refs, head, state, decay):
    decay = jnp.broadcast_to(decay, (EXTRA, E))
    high = decay.astype(BF16)
    rest = decay - high.astype(F32)
    middle = rest.astype(BF16)
    low = (rest - middle.astype(F32)).astype(BF16)
    row = lax.broadcasted_iota(jnp.int32, (EXTRA, E), 0)
    part = jnp.where(row == 0, high.astype(F32), jnp.where(row == 1, middle.astype(F32), low.astype(F32)))
    part = part.astype(BF16)
    state = state.astype(BF16)
    for ref in refs:
        ref[head, :E, :] = state
        ref[head, E:, :] = part


def read_decay(ref, head):
    rows = ref[head, E:, :].astype(F32)
    return (rows[0:1] + rows[1:2]) + rows[2:3]


def pieces_kernel(weight_ref, out_ref):
    for c in range(3):
        for i in range(NZ):
            half = slice((i % 2) * 256, (i % 2 + 1) * 256)
            out_ref[i, :, c * 256 : (c + 1) * 256] = weight_ref[c, :, half]


def order_kernel(sent_ref, out_ref):
    for s in range(2):
        for h in range(NH):
            out_ref[:, (h * 2 + s) * 256 : (h * 2 + s + 1) * 256] = sent_ref[s * NH + h]


def states_kernel(total_ref, last_ref, col_ref, row_ref, proj_ref, prefix_ref, message_ref):
    for half in range(2):
        part = slice(half * 512, (half + 1) * 512)
        proj_ref[half] = (total_ref[part] + last_ref[part]).astype(BF16)
    for head in range(2):
        state = jnp.zeros((E, E), F32)
        decay = jnp.zeros((1, 1), F32)
        for n in range(8):
            at = head * 8 + n
            rows = slice((n % 4) * BLK, (n % 4 + 1) * BLK)
            keys = proj_ref[n // 4, rows, head * E : (head + 1) * E]
            values = proj_ref[n // 4, rows, 256 + head * E : 256 + (head + 1) * E]
            last = row_ref[at : at + 1, BLK - 1 : BLK]
            scale = jnp.exp(last - col_ref[:, at : at + 1])
            prefix_ref[at] = state.astype(BF16)
            scaled = (keys.astype(F32) * scale).astype(BF16)
            state = jnp.exp(last) * state + mm(scaled, values, (((0,), (0,)), ((), ())))
            decay = decay + last
        write_message([message_ref.at[k] for k in range(4)], head, state, decay)


def local_kernel(total_ref, proj_ref, prefix_ref, col_ref, row_ref, query_ref, out_ref):
    for half in range(2):
        query_ref[half] = total_ref[half * 512 : (half + 1) * 512].astype(BF16)
    causal = lax.broadcasted_iota(jnp.int32, (BLK, BLK), 0) >= lax.broadcasted_iota(jnp.int32, (BLK, BLK), 1)
    for head in range(2):
        for n in range(8):
            at = head * 8 + n
            rows = slice((n % 4) * BLK, (n % 4 + 1) * BLK)
            queries = query_ref[n // 4, rows, head * E : (head + 1) * E]
            keys = proj_ref[n // 4, rows, head * E : (head + 1) * E]
            values = proj_ref[n // 4, rows, 256 + head * E : 256 + (head + 1) * E]
            col = col_ref[:, at : at + 1]
            gaps = col - row_ref[at : at + 1, :]
            weights = jnp.exp(jnp.where(causal, gaps, -1e30))
            scores = mm(queries, keys, (((1,), (1,)), ((), ()))) * weights
            scaled = (queries.astype(F32) * jnp.exp(col)).astype(BF16)
            out_ref[at] = mm(scores.astype(BF16), values) + mm(scaled, prefix_ref[at])


def row_kernel(place_ref, messages_ref, before_ref, decay_ref, message_ref):
    place = place_ref[0]
    for head in range(2):
        before = jnp.zeros((E, E), F32)
        total = jnp.zeros((E, E), F32)
        gone_before = jnp.zeros((1, E), F32)
        gone = jnp.zeros((1, E), F32)
        for k in (3, 2, 1, 0):
            block = messages_ref[k, head, :E, :].astype(F32)
            decay = read_decay(messages_ref.at[k], head)
            total = total + jnp.exp(gone) * block
            gone = gone + decay
            early = k < place
            before = before + jnp.where(early, jnp.exp(gone_before), 0.0) * block
            gone_before = gone_before + jnp.where(early, decay, 0.0)
        before_ref[head] = before
        decay_ref[head] = jnp.broadcast_to(gone_before, (8, E))
        write_message([message_ref], head, total, gone)


def final_kernel(*refs):
    messages = [refs[START_ORDER.index(k)] for k in range(1, NY)]
    before_ref, decay_ref, part_ref, query_ref, col_ref, start_ref, gain_ref, out_ref = refs[7:]
    for head in range(2):
        carried = jnp.zeros((E, E), F32)
        gone = jnp.zeros((1, E), F32)
        for ref in messages:
            carried = carried + jnp.exp(gone) * ref[head, :E, :].astype(F32)
            gone = gone + read_decay(ref, head)
        incoming = (jnp.exp(decay_ref[head, 0:1, :]) * carried + before_ref[head]).astype(BF16)
        gain = gain_ref[0:1, head * E : (head + 1) * E]
        for n in range(8):
            at = head * 8 + n
            rows = slice((n % 4) * BLK, (n % 4 + 1) * BLK)
            queries = query_ref[n // 4, rows, head * E : (head + 1) * E]
            scale = jnp.exp(col_ref[:, at : at + 1] + start_ref[0:1, at : at + 1])
            scaled = (queries.astype(F32) * scale).astype(BF16)
            output = part_ref[at] + mm(scaled, incoming)
            meansq = jnp.mean(output * output, axis=1, keepdims=True)
            gained = output / jnp.sqrt(meansq + EPS) * gain
            out_ref[n * BLK : (n + 1) * BLK, head * E : (head + 1) * E] = gained.astype(BF16)


def call(kernel, outs, scalars, *args, flops=0):
    shapes = [jax.ShapeDtypeStruct(s, d) for s, d in outs]
    smem = [pl.BlockSpec(memory_space=pltpu.SMEM)] * len(scalars)
    moved = sum(a.size * a.dtype.itemsize for a in args)
    return pl.pallas_call(
        kernel,
        out_shape=shapes,
        in_specs=smem + whole(len(args)),
        out_specs=whole(len(outs)),
        cost_estimate=pl.CostEstimate(flops=flops, bytes_accessed=moved, transcendentals=0),
        compiler_params=pltpu.CompilerParams(vmem_limit_bytes=32 * 1024 * 1024),
    )(*scalars, *args)


def on_device(tokens, qkv_weight, log_decay, norm_gain):
    seq = lax.axis_index("seq")
    y, z = seq // NZ, seq % NZ
    side = z % 2
    place = z // 2
    place1 = place.reshape(1).astype(jnp.int32)

    (pieces,) = call(pieces_kernel, [((NZ, 48, 768), BF16)], [], qkv_weight.transpose(1, 0, 2))
    block = lax.all_to_all(pieces, "seq", split_axis=0, concat_axis=0, tiled=True, axis_index_groups=Z_GROUPS)

    all_rows = lax.all_gather(tokens, ("seq", "head"), axis=0, tiled=True, axis_index_groups=OUT_GROUPS)


    def add(total, part, offset):
        x = lax.dynamic_slice_in_dim(all_rows, ((y + offset) % NY) * (NZ * 48), NZ * 48, 1)
        d = jnp.dot(x, part.reshape(NZ * 48, 512), preferred_element_type=F32)
        return d if total is None else total + d

    query_block = block[:, :, :256]
    block = block[:, :, 256:]
    ups, downs = [block], [block]

    def hop(*earlier):
        ups.append(lax.ppermute(after(ups[-1], *earlier), "seq", y_shift(1)))
        downs.append(lax.ppermute(after(downs[-1], *earlier), "seq", y_shift(-1)))

    def add_step(total, step):
        return add(add(total, ups[step], -step), downs[step], step)

    hop()
    mine = lax.dynamic_slice_in_dim(log_decay, side * 2, 2, 0)
    wanted = lax.dynamic_slice_in_dim(log_decay, (1 - side) * 2, 2, 0)
    theirs = lax.ppermute(after(wanted, block), "seq", PAIR)
    ups.append(lax.ppermute(ups[1], "seq", y_shift(1)))
    downs.append(lax.ppermute(after(downs[1], theirs), "seq", y_shift(-1)))
    both = jnp.where(side == 0, jnp.concatenate([mine, theirs], 1), jnp.concatenate([theirs, mine], 1))
    rows = jnp.cumsum(both.reshape(2, 8, BLK), axis=2)
    ends = rows[:, :, -1]
    starts = (jnp.cumsum(ends, axis=1) - ends).reshape(1, 16)
    rows = rows.reshape(16, BLK)
    cols = rows.T
    gain = lax.dynamic_slice_in_dim(norm_gain, side * 256, 256, 0).reshape(1, 256)

    hop(rows, cols, starts, gain)
    total = add(add(None, block, 0), ups[1], -1)
    query_weight = lax.all_gather(
        after(query_block, all_rows), "seq", axis=0, tiled=True, axis_index_groups=Y_GROUPS
    ).reshape(NY * NZ * 48, 256)
    up4 = lax.ppermute(after(ups[3], total)[:4], "seq", y_shift(1))
    down4 = lax.ppermute(after(downs[3], total)[4:], "seq", y_shift(-1))
    total = add_step(add_step(add(total, downs[1], 1), 2), 3)
    up4, down4, total = lax.optimization_barrier((up4, down4, total))
    last = add(None, jnp.concatenate([up4, down4], 0), 4)

    proj, prefix, messages = call(
        states_kernel,
        [((2, 512, 512), BF16), ((16, E, E), BF16), ((4, 2, E + EXTRA, E), BF16)],
        [], total, last, cols, rows, flops=16 * 2 * E**3,
    )
    messages = lax.all_to_all(messages, "seq", split_axis=0, concat_axis=0, tiled=True, axis_index_groups=ROW_GROUPS)
    query_total = jnp.dot(all_rows, after(query_weight, messages), preferred_element_type=F32)
    query, part = call(
        local_kernel, [((2, 512, 256), BF16), ((16, BLK, E), F32)], [], query_total, proj, prefix, cols, rows,
        flops=16 * 6 * E**3,
    )
    before, gone, row_message = call(
        row_kernel,
        [((2, E, E), F32), ((2, 8, E), F32), ((2, E + EXTRA, E), BF16)],
        [place1], messages,
    )
    earlier = [lax.ppermute(row_message, "seq", y_later(k)) for k in START_ORDER]
    (flat,) = call(
        final_kernel, [((1024, 256), BF16)], [], *earlier, before, gone, part, query, cols, starts, gain,
        flops=16 * 2 * E**3,
    )
    sent = lax.all_to_all(
        flat.reshape(16, 64, 256), ("seq", "head"), split_axis=0, concat_axis=0, tiled=True,
        axis_index_groups=OUT_GROUPS,
    )
    (out,) = call(order_kernel, [((64, 4096), BF16)], [], sent)
    return out


def solution(mesh):
    return jax.shard_map(
        on_device,
        mesh=mesh,
        in_specs=(P(("seq", "head"), None), P("seq", None, "head"), P("head", "seq"), P("head")),
        out_specs=P(("seq", "head"), None),
        check_vma=False,
    )
```

```python
import functools

import jax
import jax.numpy as jnp
from jax import lax
from jax.experimental import pallas as pl
from jax.experimental.pallas import tpu as pltpu
from jax.sharding import PartitionSpec as P

BLK = 128
E = 128
EPS = 1e-05
NY = 8
NZ = 8
NH = 8
EXTRA = 16
START_ORDER = (1, 2, 4, 5, 3, 6, 7)
F32 = jnp.float32
BF16 = jnp.bfloat16
VMEM = pltpu.VMEM

Z_GROUPS = [[y * NZ + z for z in range(NZ)] for y in range(NY)]
Y_GROUPS = [[y * NZ + z for y in range(NY)] for z in range(NZ)]
ROW_GROUPS = [[y * NZ + p + 2 * i for i in range(4)] for y in range(NY) for p in range(2)]
OUT_GROUPS = [[g * 16 + i for i in range(16)] for g in range(NY * NZ // 2)]


def y_shift(d):
    return [(y * NZ + z, ((y + d) % NY) * NZ + z) for y in range(NY) for z in range(NZ)]


def y_later(d):
    return [(y * NZ + z, (y + d) * NZ + z) for y in range(NY - d) for z in range(NZ)]


PAIR = [(s, s ^ 1) for s in range(NY * NZ)]


def after(value, *earlier):
    return lax.optimization_barrier((value,) + earlier)[0]


def whole(count):
    return [pl.BlockSpec(memory_space=VMEM)] * count


def mm(a, b, dims=(((1,), (0,)), ((), ()))):
    return lax.dot_general(a, b, dims, preferred_element_type=F32)


def write_message(refs, head, state, decay):
    decay = jnp.broadcast_to(decay, (EXTRA, E))
    high = decay.astype(BF16)
    rest = decay - high.astype(F32)
    middle = rest.astype(BF16)
    low = (rest - middle.astype(F32)).astype(BF16)
    row = lax.broadcasted_iota(jnp.int32, (EXTRA, E), 0)
    part = jnp.where(row == 0, high.astype(F32), jnp.where(row == 1, middle.astype(F32), low.astype(F32)))
    part = part.astype(BF16)
    state = state.astype(BF16)
    for ref in refs:
        ref[head, :E, :] = state
        ref[head, E:, :] = part


def read_decay(ref, head):
    rows = ref[head, E:, :].astype(F32)
    return (rows[0:1] + rows[1:2]) + rows[2:3]


def pieces_kernel(weight_ref, out_ref):
    for c in range(3):
        for i in range(NZ):
            half = slice((i % 2) * 256, (i % 2 + 1) * 256)
            out_ref[i, :, c * 256 : (c + 1) * 256] = weight_ref[c, :, half]


def order_kernel(sent_ref, out_ref):
    for s in range(2):
        for h in range(NH):
            out_ref[:, (h * 2 + s) * 256 : (h * 2 + s + 1) * 256] = sent_ref[s * NH + h]


def states_kernel(total_ref, last_ref, col_ref, row_ref, proj_ref, prefix_ref, message_ref):
    for half in range(2):
        part = slice(half * 512, (half + 1) * 512)
        proj_ref[half] = (total_ref[part] + last_ref[part]).astype(BF16)
    for head in range(2):
        state = jnp.zeros((E, E), F32)
        decay = jnp.zeros((1, 1), F32)
        for n in range(8):
            at = head * 8 + n
            rows = slice((n % 4) * BLK, (n % 4 + 1) * BLK)
            keys = proj_ref[n // 4, rows, head * E : (head + 1) * E]
            values = proj_ref[n // 4, rows, 256 + head * E : 256 + (head + 1) * E]
            last = row_ref[at : at + 1, BLK - 1 : BLK]
            scale = jnp.exp(last - col_ref[:, at : at + 1])
            prefix_ref[at] = state.astype(BF16)
            scaled = (keys.astype(F32) * scale).astype(BF16)
            state = jnp.exp(last) * state + mm(scaled, values, (((0,), (0,)), ((), ())))
            decay = decay + last
        write_message([message_ref.at[k] for k in range(4)], head, state, decay)


def local_kernel(total_ref, proj_ref, prefix_ref, col_ref, row_ref, query_ref, out_ref):
    for half in range(2):
        query_ref[half] = total_ref[half * 512 : (half + 1) * 512].astype(BF16)
    causal = lax.broadcasted_iota(jnp.int32, (BLK, BLK), 0) >= lax.broadcasted_iota(jnp.int32, (BLK, BLK), 1)
    for head in range(2):
        for n in range(8):
            at = head * 8 + n
            rows = slice((n % 4) * BLK, (n % 4 + 1) * BLK)
            queries = query_ref[n // 4, rows, head * E : (head + 1) * E]
            keys = proj_ref[n // 4, rows, head * E : (head + 1) * E]
            values = proj_ref[n // 4, rows, 256 + head * E : 256 + (head + 1) * E]
            col = col_ref[:, at : at + 1]
            gaps = col - row_ref[at : at + 1, :]
            weights = jnp.exp(jnp.where(causal, gaps, -1e30))
            scores = mm(queries, keys, (((1,), (1,)), ((), ()))) * weights
            scaled = (queries.astype(F32) * jnp.exp(col)).astype(BF16)
            out_ref[at] = mm(scores.astype(BF16), values) + mm(scaled, prefix_ref[at])


def row_kernel(place_ref, messages_ref, before_ref, decay_ref, message_ref):
    place = place_ref[0]
    for head in range(2):
        before = jnp.zeros((E, E), F32)
        total = jnp.zeros((E, E), F32)
        gone_before = jnp.zeros((1, E), F32)
        gone = jnp.zeros((1, E), F32)
        for k in (3, 2, 1, 0):
            block = messages_ref[k, head, :E, :].astype(F32)
            decay = read_decay(messages_ref.at[k], head)
            total = total + jnp.exp(gone) * block
            gone = gone + decay
            early = k < place
            before = before + jnp.where(early, jnp.exp(gone_before), 0.0) * block
            gone_before = gone_before + jnp.where(early, decay, 0.0)
        before_ref[head] = before
        decay_ref[head] = jnp.broadcast_to(gone_before, (8, E))
        write_message([message_ref], head, total, gone)


def final_kernel(*refs):
    messages = [refs[START_ORDER.index(k)] for k in range(1, NY)]
    before_ref, decay_ref, part_ref, query_ref, col_ref, start_ref, gain_ref, out_ref = refs[7:]
    for head in range(2):
        carried = jnp.zeros((E, E), F32)
        gone = jnp.zeros((1, E), F32)
        for ref in messages:
            carried = carried + jnp.exp(gone) * ref[head, :E, :].astype(F32)
            gone = gone + read_decay(ref, head)
        incoming = (jnp.exp(decay_ref[head, 0:1, :]) * carried + before_ref[head]).astype(BF16)
        gain = gain_ref[0:1, head * E : (head + 1) * E]
        for n in range(8):
            at = head * 8 + n
            rows = slice((n % 4) * BLK, (n % 4 + 1) * BLK)
            queries = query_ref[n // 4, rows, head * E : (head + 1) * E]
            scale = jnp.exp(col_ref[:, at : at + 1] + start_ref[0:1, at : at + 1])
            scaled = (queries.astype(F32) * scale).astype(BF16)
            output = part_ref[at] + mm(scaled, incoming)
            meansq = jnp.mean(output * output, axis=1, keepdims=True)
            gained = output * (1.0 / jnp.sqrt(meansq + EPS)) * gain
            out_ref[n * BLK : (n + 1) * BLK, head * E : (head + 1) * E] = gained.astype(BF16)


def call(kernel, outs, scalars, *args, flops=0):
    shapes = [jax.ShapeDtypeStruct(s, d) for s, d in outs]
    smem = [pl.BlockSpec(memory_space=pltpu.SMEM)] * len(scalars)
    moved = sum(a.size * a.dtype.itemsize for a in args)
    return pl.pallas_call(
        kernel,
        out_shape=shapes,
        in_specs=smem + whole(len(args)),
        out_specs=whole(len(outs)),
        cost_estimate=pl.CostEstimate(flops=flops, bytes_accessed=moved, transcendentals=0),
        compiler_params=pltpu.CompilerParams(vmem_limit_bytes=32 * 1024 * 1024),
    )(*scalars, *args)


def on_device(tokens, qkv_weight, log_decay, norm_gain):
    seq = lax.axis_index("seq")
    y, z = seq // NZ, seq % NZ
    side = z % 2
    place = z // 2
    place1 = place.reshape(1).astype(jnp.int32)

    (pieces,) = call(pieces_kernel, [((NZ, 48, 768), BF16)], [], qkv_weight.transpose(1, 0, 2))
    block = lax.all_to_all(pieces, "seq", split_axis=0, concat_axis=0, tiled=True, axis_index_groups=Z_GROUPS)

    all_rows = lax.all_gather(tokens, ("seq", "head"), axis=0, tiled=True, axis_index_groups=OUT_GROUPS)


    def add(total, part, offset):
        x = lax.dynamic_slice_in_dim(all_rows, ((y + offset) % NY) * (NZ * 48), NZ * 48, 1)
        d = jnp.dot(x, part.reshape(NZ * 48, 512), preferred_element_type=F32)
        return d if total is None else total + d

    query_block = block[:, :, :256]
    block = block[:, :, 256:]
    ups, downs = [block], [block]

    def hop(*earlier):
        ups.append(lax.ppermute(after(ups[-1], *earlier), "seq", y_shift(1)))
        downs.append(lax.ppermute(after(downs[-1], *earlier), "seq", y_shift(-1)))

    def add_step(total, step):
        return add(add(total, ups[step], -step), downs[step], step)

    hop()
    mine = lax.dynamic_slice_in_dim(log_decay, side * 2, 2, 0)
    wanted = lax.dynamic_slice_in_dim(log_decay, (1 - side) * 2, 2, 0)
    theirs = lax.ppermute(after(wanted, block), "seq", PAIR)
    ups.append(lax.ppermute(ups[1], "seq", y_shift(1)))
    downs.append(lax.ppermute(after(downs[1], theirs), "seq", y_shift(-1)))
    both = jnp.where(side == 0, jnp.concatenate([mine, theirs], 1), jnp.concatenate([theirs, mine], 1))
    rows = jnp.cumsum(both.reshape(2, 8, BLK), axis=2)
    ends = rows[:, :, -1]
    starts = (jnp.cumsum(ends, axis=1) - ends).reshape(1, 16)
    rows = rows.reshape(16, BLK)
    cols = rows.T
    gain = lax.dynamic_slice_in_dim(norm_gain, side * 256, 256, 0).reshape(1, 256)

    hop(rows, cols, starts, gain)
    total = add(add(None, block, 0), ups[1], -1)
    query_weight = lax.all_gather(
        after(query_block, all_rows), "seq", axis=0, tiled=True, axis_index_groups=Y_GROUPS
    ).reshape(NY * NZ * 48, 256)
    up4 = lax.ppermute(after(ups[3], total)[:4], "seq", y_shift(1))
    down4 = lax.ppermute(after(downs[3], total)[4:], "seq", y_shift(-1))
    total = add_step(add_step(add(total, downs[1], 1), 2), 3)
    up4, down4, total = lax.optimization_barrier((up4, down4, total))
    last = add(None, jnp.concatenate([up4, down4], 0), 4)

    proj, prefix, messages = call(
        states_kernel,
        [((2, 512, 512), BF16), ((16, E, E), BF16), ((4, 2, E + EXTRA, E), BF16)],
        [], total, last, cols, rows, flops=16 * 2 * E**3,
    )
    messages = lax.all_to_all(messages, "seq", split_axis=0, concat_axis=0, tiled=True, axis_index_groups=ROW_GROUPS)
    query_total = jnp.dot(all_rows, after(query_weight, messages), preferred_element_type=F32)
    query, part = call(
        local_kernel, [((2, 512, 256), BF16), ((16, BLK, E), F32)], [], query_total, proj, prefix, cols, rows,
        flops=16 * 6 * E**3,
    )
    before, gone, row_message = call(
        row_kernel,
        [((2, E, E), F32), ((2, 8, E), F32), ((2, E + EXTRA, E), BF16)],
        [place1], messages,
    )
    earlier = [lax.ppermute(row_message, "seq", y_later(k)) for k in START_ORDER]
    (flat,) = call(
        final_kernel, [((1024, 256), BF16)], [], *earlier, before, gone, part, query, cols, starts, gain,
        flops=16 * 2 * E**3,
    )
    sent = lax.all_to_all(
        flat.reshape(16, 64, 256), ("seq", "head"), split_axis=0, concat_axis=0, tiled=True,
        axis_index_groups=OUT_GROUPS,
    )
    (out,) = call(order_kernel, [((64, 4096), BF16)], [], sent)
    return out


def solution(mesh):
    return jax.shard_map(
        on_device,
        mesh=mesh,
        in_specs=(P(("seq", "head"), None), P("seq", None, "head"), P("head", "seq"), P("head")),
        out_specs=P(("seq", "head"), None),
        check_vma=False,
    )
```

```python
import functools

import jax
import jax.numpy as jnp
from jax import lax
from jax.experimental import pallas as pl
from jax.experimental.pallas import tpu as pltpu
from jax.sharding import PartitionSpec as P

BLK = 128
E = 128
EPS = 1e-05
NY = 8
NZ = 8
NH = 8
EXTRA = 16
START_ORDER = (1, 2, 4, 5, 6, 3, 7)
F32 = jnp.float32
BF16 = jnp.bfloat16
VMEM = pltpu.VMEM

Z_GROUPS = [[y * NZ + z for z in range(NZ)] for y in range(NY)]
Y_GROUPS = [[y * NZ + z for y in range(NY)] for z in range(NZ)]
ROW_GROUPS = [[y * NZ + p + 2 * i for i in range(4)] for y in range(NY) for p in range(2)]
OUT_GROUPS = [[g * 16 + i for i in range(16)] for g in range(NY * NZ // 2)]


def y_shift(d):
    return [(y * NZ + z, ((y + d) % NY) * NZ + z) for y in range(NY) for z in range(NZ)]


def y_later(d):
    return [(y * NZ + z, (y + d) * NZ + z) for y in range(NY - d) for z in range(NZ)]


PAIR = [(s, s ^ 1) for s in range(NY * NZ)]


def after(value, *earlier):
    return lax.optimization_barrier((value,) + earlier)[0]


def whole(count):
    return [pl.BlockSpec(memory_space=VMEM)] * count


def mm(a, b, dims=(((1,), (0,)), ((), ()))):
    return lax.dot_general(a, b, dims, preferred_element_type=F32)


def write_message(refs, head, state, decay):
    decay = jnp.broadcast_to(decay, (EXTRA, E))
    high = decay.astype(BF16)
    rest = decay - high.astype(F32)
    middle = rest.astype(BF16)
    low = (rest - middle.astype(F32)).astype(BF16)
    row = lax.broadcasted_iota(jnp.int32, (EXTRA, E), 0)
    part = jnp.where(row == 0, high.astype(F32), jnp.where(row == 1, middle.astype(F32), low.astype(F32)))
    part = part.astype(BF16)
    state = state.astype(BF16)
    for ref in refs:
        ref[head, :E, :] = state
        ref[head, E:, :] = part


def read_decay(ref, head):
    rows = ref[head, E:, :].astype(F32)
    return (rows[0:1] + rows[1:2]) + rows[2:3]


def pieces_kernel(weight_ref, out_ref):
    for c in range(3):
        for i in range(NZ):
            half = slice((i % 2) * 256, (i % 2 + 1) * 256)
            out_ref[i, :, c * 256 : (c + 1) * 256] = weight_ref[c, :, half]


def order_kernel(sent_ref, out_ref):
    for s in range(2):
        for h in range(NH):
            out_ref[:, (h * 2 + s) * 256 : (h * 2 + s + 1) * 256] = sent_ref[s * NH + h]


def states_kernel(total_ref, last_ref, col_ref, row_ref, proj_ref, prefix_ref, message_ref):
    for half in range(2):
        part = slice(half * 512, (half + 1) * 512)
        proj_ref[half] = (total_ref[part] + last_ref[part]).astype(BF16)
    for head in range(2):
        state = jnp.zeros((E, E), F32)
        decay = jnp.zeros((1, 1), F32)
        for n in range(8):
            at = head * 8 + n
            rows = slice((n % 4) * BLK, (n % 4 + 1) * BLK)
            keys = proj_ref[n // 4, rows, head * E : (head + 1) * E]
            values = proj_ref[n // 4, rows, 256 + head * E : 256 + (head + 1) * E]
            last = row_ref[at : at + 1, BLK - 1 : BLK]
            scale = jnp.exp(last - col_ref[:, at : at + 1])
            prefix_ref[at] = state.astype(BF16)
            scaled = (keys.astype(F32) * scale).astype(BF16)
            state = jnp.exp(last) * state + mm(scaled, values, (((0,), (0,)), ((), ())))
            decay = decay + last
        write_message([message_ref.at[k] for k in range(4)], head, state, decay)


def local_kernel(total_ref, proj_ref, prefix_ref, col_ref, row_ref, query_ref, out_ref):
    for half in range(2):
        query_ref[half] = total_ref[half * 512 : (half + 1) * 512].astype(BF16)
    causal = lax.broadcasted_iota(jnp.int32, (BLK, BLK), 0) >= lax.broadcasted_iota(jnp.int32, (BLK, BLK), 1)
    for head in range(2):
        for n in range(8):
            at = head * 8 + n
            rows = slice((n % 4) * BLK, (n % 4 + 1) * BLK)
            queries = query_ref[n // 4, rows, head * E : (head + 1) * E]
            keys = proj_ref[n // 4, rows, head * E : (head + 1) * E]
            values = proj_ref[n // 4, rows, 256 + head * E : 256 + (head + 1) * E]
            col = col_ref[:, at : at + 1]
            gaps = col - row_ref[at : at + 1, :]
            weights = jnp.exp(jnp.where(causal, gaps, -1e30))
            scores = mm(queries, keys, (((1,), (1,)), ((), ()))) * weights
            scaled = (queries.astype(F32) * jnp.exp(col)).astype(BF16)
            out_ref[at] = mm(scores.astype(BF16), values) + mm(scaled, prefix_ref[at])


def row_kernel(place_ref, messages_ref, before_ref, decay_ref, message_ref):
    place = place_ref[0]
    for head in range(2):
        before = jnp.zeros((E, E), F32)
        total = jnp.zeros((E, E), F32)
        gone_before = jnp.zeros((1, E), F32)
        gone = jnp.zeros((1, E), F32)
        for k in (3, 2, 1, 0):
            block = messages_ref[k, head, :E, :].astype(F32)
            decay = read_decay(messages_ref.at[k], head)
            total = total + jnp.exp(gone) * block
            gone = gone + decay
            early = k < place
            before = before + jnp.where(early, jnp.exp(gone_before), 0.0) * block
            gone_before = gone_before + jnp.where(early, decay, 0.0)
        before_ref[head] = before
        decay_ref[head] = jnp.broadcast_to(gone_before, (8, E))
        write_message([message_ref], head, total, gone)


def final_kernel(*refs):
    messages = [refs[START_ORDER.index(k)] for k in range(1, NY)]
    before_ref, decay_ref, part_ref, query_ref, col_ref, start_ref, gain_ref, out_ref = refs[7:]
    for head in range(2):
        carried = jnp.zeros((E, E), F32)
        gone = jnp.zeros((1, E), F32)
        for ref in messages:
            carried = carried + jnp.exp(gone) * ref[head, :E, :].astype(F32)
            gone = gone + read_decay(ref, head)
        incoming = (jnp.exp(decay_ref[head, 0:1, :]) * carried + before_ref[head]).astype(BF16)
        gain = gain_ref[0:1, head * E : (head + 1) * E]
        for n in range(8):
            at = head * 8 + n
            rows = slice((n % 4) * BLK, (n % 4 + 1) * BLK)
            queries = query_ref[n // 4, rows, head * E : (head + 1) * E]
            scale = jnp.exp(col_ref[:, at : at + 1] + start_ref[0:1, at : at + 1])
            scaled = (queries.astype(F32) * scale).astype(BF16)
            output = part_ref[at] + mm(scaled, incoming)
            meansq = jnp.mean(output * output, axis=1, keepdims=True)
            gained = output / jnp.sqrt(meansq + EPS) * gain
            out_ref[n * BLK : (n + 1) * BLK, head * E : (head + 1) * E] = gained.astype(BF16)


def call(kernel, outs, scalars, *args, flops=0):
    shapes = [jax.ShapeDtypeStruct(s, d) for s, d in outs]
    smem = [pl.BlockSpec(memory_space=pltpu.SMEM)] * len(scalars)
    moved = sum(a.size * a.dtype.itemsize for a in args)
    return pl.pallas_call(
        kernel,
        out_shape=shapes,
        in_specs=smem + whole(len(args)),
        out_specs=whole(len(outs)),
        cost_estimate=pl.CostEstimate(flops=flops, bytes_accessed=moved, transcendentals=0),
        compiler_params=pltpu.CompilerParams(vmem_limit_bytes=32 * 1024 * 1024),
    )(*scalars, *args)


def on_device(tokens, qkv_weight, log_decay, norm_gain):
    seq = lax.axis_index("seq")
    y, z = seq // NZ, seq % NZ
    side = z % 2
    place = z // 2
    place1 = place.reshape(1).astype(jnp.int32)

    (pieces,) = call(pieces_kernel, [((NZ, 48, 768), BF16)], [], qkv_weight.transpose(1, 0, 2))
    block = lax.all_to_all(pieces, "seq", split_axis=0, concat_axis=0, tiled=True, axis_index_groups=Z_GROUPS)

    all_rows = lax.all_gather(tokens, ("seq", "head"), axis=0, tiled=True, axis_index_groups=OUT_GROUPS)


    def add(total, part, offset):
        x = lax.dynamic_slice_in_dim(all_rows, ((y + offset) % NY) * (NZ * 48), NZ * 48, 1)
        d = jnp.dot(x, part.reshape(NZ * 48, 512), preferred_element_type=F32)
        return d if total is None else total + d

    query_block = block[:, :, :256]
    block = block[:, :, 256:]
    ups, downs = [block], [block]

    def hop(*earlier):
        ups.append(lax.ppermute(after(ups[-1], *earlier), "seq", y_shift(1)))
        downs.append(lax.ppermute(after(downs[-1], *earlier), "seq", y_shift(-1)))

    def add_step(total, step):
        return add(add(total, ups[step], -step), downs[step], step)

    hop()
    mine = lax.dynamic_slice_in_dim(log_decay, side * 2, 2, 0)
    wanted = lax.dynamic_slice_in_dim(log_decay, (1 - side) * 2, 2, 0)
    theirs = lax.ppermute(after(wanted, block), "seq", PAIR)
    ups.append(lax.ppermute(ups[1], "seq", y_shift(1)))
    downs.append(lax.ppermute(after(downs[1], theirs), "seq", y_shift(-1)))
    both = jnp.where(side == 0, jnp.concatenate([mine, theirs], 1), jnp.concatenate([theirs, mine], 1))
    rows = jnp.cumsum(both.reshape(2, 8, BLK), axis=2)
    ends = rows[:, :, -1]
    starts = (jnp.cumsum(ends, axis=1) - ends).reshape(1, 16)
    rows = rows.reshape(16, BLK)
    cols = rows.T
    gain = lax.dynamic_slice_in_dim(norm_gain, side * 256, 256, 0).reshape(1, 256)

    hop(rows, cols, starts, gain)
    total = add(add(None, block, 0), ups[1], -1)
    query_weight = lax.all_gather(
        after(query_block, all_rows), "seq", axis=0, tiled=True, axis_index_groups=Y_GROUPS
    ).reshape(NY * NZ * 48, 256)
    up4 = lax.ppermute(after(ups[3], total)[:4], "seq", y_shift(1))
    down4 = lax.ppermute(after(downs[3], total)[4:], "seq", y_shift(-1))
    total = add_step(add_step(add(total, downs[1], 1), 2), 3)
    up4, down4, total = lax.optimization_barrier((up4, down4, total))
    last = add(None, jnp.concatenate([up4, down4], 0), 4)

    proj, prefix, messages = call(
        states_kernel,
        [((2, 512, 512), BF16), ((16, E, E), BF16), ((4, 2, E + EXTRA, E), BF16)],
        [], total, last, cols, rows, flops=16 * 2 * E**3,
    )
    messages = lax.all_to_all(messages, "seq", split_axis=0, concat_axis=0, tiled=True, axis_index_groups=ROW_GROUPS)
    query_total = jnp.dot(all_rows, after(query_weight, messages), preferred_element_type=F32)
    query, part = call(
        local_kernel, [((2, 512, 256), BF16), ((16, BLK, E), F32)], [], query_total, proj, prefix, cols, rows,
        flops=16 * 6 * E**3,
    )
    before, gone, row_message = call(
        row_kernel,
        [((2, E, E), F32), ((2, 8, E), F32), ((2, E + EXTRA, E), BF16)],
        [place1], messages,
    )
    earlier = [lax.ppermute(row_message, "seq", y_later(k)) for k in START_ORDER]
    (flat,) = call(
        final_kernel, [((1024, 256), BF16)], [], *earlier, before, gone, part, query, cols, starts, gain,
        flops=16 * 2 * E**3,
    )
    sent = lax.all_to_all(
        flat.reshape(16, 64, 256), ("seq", "head"), split_axis=0, concat_axis=0, tiled=True,
        axis_index_groups=OUT_GROUPS,
    )
    (out,) = call(order_kernel, [((64, 4096), BF16)], [], sent)
    return out


def solution(mesh):
    return jax.shard_map(
        on_device,
        mesh=mesh,
        in_specs=(P(("seq", "head"), None), P("seq", None, "head"), P("head", "seq"), P("head")),
        out_specs=P(("seq", "head"), None),
        check_vma=False,
    )
```

```python
import functools

import jax
import jax.numpy as jnp
from jax import lax
from jax.experimental import pallas as pl
from jax.experimental.pallas import tpu as pltpu
from jax.sharding import PartitionSpec as P

BLK = 128
E = 128
EPS = 1e-05
NY = 8
NZ = 8
NH = 8
EXTRA = 16
START_ORDER = (1, 2, 7, 6, 5, 4, 3)
F32 = jnp.float32
BF16 = jnp.bfloat16
VMEM = pltpu.VMEM

Z_GROUPS = [[y * NZ + z for z in range(NZ)] for y in range(NY)]
Y_GROUPS = [[y * NZ + z for y in range(NY)] for z in range(NZ)]
ROW_GROUPS = [[y * NZ + p + 2 * i for i in range(4)] for y in range(NY) for p in range(2)]
OUT_GROUPS = [[g * 16 + i for i in range(16)] for g in range(NY * NZ // 2)]


def y_shift(d):
    return [(y * NZ + z, ((y + d) % NY) * NZ + z) for y in range(NY) for z in range(NZ)]


def y_later(d):
    return [(y * NZ + z, (y + d) * NZ + z) for y in range(NY - d) for z in range(NZ)]


PAIR = [(s, s ^ 1) for s in range(NY * NZ)]


def after(value, *earlier):
    return lax.optimization_barrier((value,) + earlier)[0]


def whole(count):
    return [pl.BlockSpec(memory_space=VMEM)] * count


def mm(a, b, dims=(((1,), (0,)), ((), ()))):
    return lax.dot_general(a, b, dims, preferred_element_type=F32)


def write_message(refs, head, state, decay):
    decay = jnp.broadcast_to(decay, (EXTRA, E))
    high = decay.astype(BF16)
    rest = decay - high.astype(F32)
    middle = rest.astype(BF16)
    low = (rest - middle.astype(F32)).astype(BF16)
    row = lax.broadcasted_iota(jnp.int32, (EXTRA, E), 0)
    part = jnp.where(row == 0, high.astype(F32), jnp.where(row == 1, middle.astype(F32), low.astype(F32)))
    part = part.astype(BF16)
    state = state.astype(BF16)
    for ref in refs:
        ref[head, :E, :] = state
        ref[head, E:, :] = part


def read_decay(ref, head):
    rows = ref[head, E:, :].astype(F32)
    return (rows[0:1] + rows[1:2]) + rows[2:3]


def pieces_kernel(weight_ref, out_ref):
    for c in range(3):
        for i in range(NZ):
            half = slice((i % 2) * 256, (i % 2 + 1) * 256)
            out_ref[i, :, c * 256 : (c + 1) * 256] = weight_ref[c, :, half]


def order_kernel(sent_ref, out_ref):
    for s in range(2):
        for h in range(NH):
            out_ref[:, (h * 2 + s) * 256 : (h * 2 + s + 1) * 256] = sent_ref[s * NH + h]


def states_kernel(total_ref, last_ref, col_ref, row_ref, proj_ref, prefix_ref, message_ref):
    for half in range(2):
        part = slice(half * 512, (half + 1) * 512)
        proj_ref[half] = (total_ref[part] + last_ref[part]).astype(BF16)
    for head in range(2):
        state = jnp.zeros((E, E), F32)
        decay = jnp.zeros((1, 1), F32)
        for n in range(8):
            at = head * 8 + n
            rows = slice((n % 4) * BLK, (n % 4 + 1) * BLK)
            keys = proj_ref[n // 4, rows, head * E : (head + 1) * E]
            values = proj_ref[n // 4, rows, 256 + head * E : 256 + (head + 1) * E]
            last = row_ref[at : at + 1, BLK - 1 : BLK]
            scale = jnp.exp(last - col_ref[:, at : at + 1])
            prefix_ref[at] = state.astype(BF16)
            scaled = (keys.astype(F32) * scale).astype(BF16)
            state = jnp.exp(last) * state + mm(scaled, values, (((0,), (0,)), ((), ())))
            decay = decay + last
        write_message([message_ref.at[k] for k in range(4)], head, state, decay)


def local_kernel(total_ref, proj_ref, prefix_ref, col_ref, row_ref, query_ref, out_ref):
    for half in range(2):
        query_ref[half] = total_ref[half * 512 : (half + 1) * 512].astype(BF16)
    causal = lax.broadcasted_iota(jnp.int32, (BLK, BLK), 0) >= lax.broadcasted_iota(jnp.int32, (BLK, BLK), 1)
    for head in range(2):
        for n in range(8):
            at = head * 8 + n
            rows = slice((n % 4) * BLK, (n % 4 + 1) * BLK)
            queries = query_ref[n // 4, rows, head * E : (head + 1) * E]
            keys = proj_ref[n // 4, rows, head * E : (head + 1) * E]
            values = proj_ref[n // 4, rows, 256 + head * E : 256 + (head + 1) * E]
            col = col_ref[:, at : at + 1]
            gaps = col - row_ref[at : at + 1, :]
            weights = jnp.exp(jnp.where(causal, gaps, -1e30))
            scores = mm(queries, keys, (((1,), (1,)), ((), ()))) * weights
            scaled = (queries.astype(F32) * jnp.exp(col)).astype(BF16)
            out_ref[at] = mm(scores.astype(BF16), values) + mm(scaled, prefix_ref[at])


def row_kernel(place_ref, messages_ref, before_ref, decay_ref, message_ref):
    place = place_ref[0]
    for head in range(2):
        before = jnp.zeros((E, E), F32)
        total = jnp.zeros((E, E), F32)
        gone_before = jnp.zeros((1, E), F32)
        gone = jnp.zeros((1, E), F32)
        for k in (3, 2, 1, 0):
            block = messages_ref[k, head, :E, :].astype(F32)
            decay = read_decay(messages_ref.at[k], head)
            total = total + jnp.exp(gone) * block
            gone = gone + decay
            early = k < place
            before = before + jnp.where(early, jnp.exp(gone_before), 0.0) * block
            gone_before = gone_before + jnp.where(early, decay, 0.0)
        before_ref[head] = before
        decay_ref[head] = jnp.broadcast_to(gone_before, (8, E))
        write_message([message_ref], head, total, gone)


def final_kernel(*refs):
    messages = [refs[START_ORDER.index(k)] for k in range(1, NY)]
    before_ref, decay_ref, part_ref, query_ref, col_ref, start_ref, gain_ref, out_ref = refs[7:]
    for head in range(2):
        carried = jnp.zeros((E, E), F32)
        gone = jnp.zeros((1, E), F32)
        for ref in messages:
            carried = carried + jnp.exp(gone) * ref[head, :E, :].astype(F32)
            gone = gone + read_decay(ref, head)
        incoming = (jnp.exp(decay_ref[head, 0:1, :]) * carried + before_ref[head]).astype(BF16)
        gain = gain_ref[0:1, head * E : (head + 1) * E]
        for n in range(8):
            at = head * 8 + n
            rows = slice((n % 4) * BLK, (n % 4 + 1) * BLK)
            queries = query_ref[n // 4, rows, head * E : (head + 1) * E]
            scale = jnp.exp(col_ref[:, at : at + 1] + start_ref[0:1, at : at + 1])
            scaled = (queries.astype(F32) * scale).astype(BF16)
            output = part_ref[at] + mm(scaled, incoming)
            meansq = jnp.mean(output * output, axis=1, keepdims=True)
            gained = output / jnp.sqrt(meansq + EPS) * gain
            out_ref[n * BLK : (n + 1) * BLK, head * E : (head + 1) * E] = gained.astype(BF16)


def call(kernel, outs, scalars, *args, flops=0):
    shapes = [jax.ShapeDtypeStruct(s, d) for s, d in outs]
    smem = [pl.BlockSpec(memory_space=pltpu.SMEM)] * len(scalars)
    moved = sum(a.size * a.dtype.itemsize for a in args)
    return pl.pallas_call(
        kernel,
        out_shape=shapes,
        in_specs=smem + whole(len(args)),
        out_specs=whole(len(outs)),
        cost_estimate=pl.CostEstimate(flops=flops, bytes_accessed=moved, transcendentals=0),
        compiler_params=pltpu.CompilerParams(vmem_limit_bytes=32 * 1024 * 1024),
    )(*scalars, *args)


def on_device(tokens, qkv_weight, log_decay, norm_gain):
    seq = lax.axis_index("seq")
    y, z = seq // NZ, seq % NZ
    side = z % 2
    place = z // 2
    place1 = place.reshape(1).astype(jnp.int32)

    (pieces,) = call(pieces_kernel, [((NZ, 48, 768), BF16)], [], qkv_weight.transpose(1, 0, 2))
    block = lax.all_to_all(pieces, "seq", split_axis=0, concat_axis=0, tiled=True, axis_index_groups=Z_GROUPS)

    all_rows = lax.all_gather(tokens, ("seq", "head"), axis=0, tiled=True, axis_index_groups=OUT_GROUPS)


    def add(total, part, offset):
        x = lax.dynamic_slice_in_dim(all_rows, ((y + offset) % NY) * (NZ * 48), NZ * 48, 1)
        d = jnp.dot(x, part.reshape(NZ * 48, 512), preferred_element_type=F32)
        return d if total is None else total + d

    query_block = block[:, :, :256]
    block = block[:, :, 256:]
    ups, downs = [block], [block]

    def hop(*earlier):
        ups.append(lax.ppermute(after(ups[-1], *earlier), "seq", y_shift(1)))
        downs.append(lax.ppermute(after(downs[-1], *earlier), "seq", y_shift(-1)))

    def add_step(total, step):
        return add(add(total, ups[step], -step), downs[step], step)

    hop()
    mine = lax.dynamic_slice_in_dim(log_decay, side * 2, 2, 0)
    wanted = lax.dynamic_slice_in_dim(log_decay, (1 - side) * 2, 2, 0)
    theirs = lax.ppermute(after(wanted, block), "seq", PAIR)
    ups.append(lax.ppermute(ups[1], "seq", y_shift(1)))
    downs.append(lax.ppermute(after(downs[1], theirs), "seq", y_shift(-1)))
    both = jnp.where(side == 0, jnp.concatenate([mine, theirs], 1), jnp.concatenate([theirs, mine], 1))
    rows = jnp.cumsum(both.reshape(2, 8, BLK), axis=2)
    ends = rows[:, :, -1]
    starts = (jnp.cumsum(ends, axis=1) - ends).reshape(1, 16)
    rows = rows.reshape(16, BLK)
    cols = rows.T
    gain = lax.dynamic_slice_in_dim(norm_gain, side * 256, 256, 0).reshape(1, 256)

    hop(rows, cols, starts, gain)
    total = add(add(None, block, 0), ups[1], -1)
    query_weight = lax.all_gather(
        after(query_block, all_rows), "seq", axis=0, tiled=True, axis_index_groups=Y_GROUPS
    ).reshape(NY * NZ * 48, 256)
    up4 = lax.ppermute(after(ups[3], total)[:4], "seq", y_shift(1))
    down4 = lax.ppermute(after(downs[3], total)[4:], "seq", y_shift(-1))
    total = add_step(add_step(add(total, downs[1], 1), 2), 3)
    up4, down4, total = lax.optimization_barrier((up4, down4, total))
    last = add(None, jnp.concatenate([up4, down4], 0), 4)

    proj, prefix, messages = call(
        states_kernel,
        [((2, 512, 512), BF16), ((16, E, E), BF16), ((4, 2, E + EXTRA, E), BF16)],
        [], total, last, cols, rows, flops=16 * 2 * E**3,
    )
    messages = lax.all_to_all(messages, "seq", split_axis=0, concat_axis=0, tiled=True, axis_index_groups=ROW_GROUPS)
    query_total = jnp.dot(all_rows, after(query_weight, messages), preferred_element_type=F32)
    query, part = call(
        local_kernel, [((2, 512, 256), BF16), ((16, BLK, E), F32)], [], query_total, proj, prefix, cols, rows,
        flops=16 * 6 * E**3,
    )
    before, gone, row_message = call(
        row_kernel,
        [((2, E, E), F32), ((2, 8, E), F32), ((2, E + EXTRA, E), BF16)],
        [place1], messages,
    )
    earlier = [lax.ppermute(row_message, "seq", y_later(k)) for k in START_ORDER]
    (flat,) = call(
        final_kernel, [((1024, 256), BF16)], [], *earlier, before, gone, part, query, cols, starts, gain,
        flops=16 * 2 * E**3,
    )
    sent = lax.all_to_all(
        flat.reshape(16, 64, 256), ("seq", "head"), split_axis=0, concat_axis=0, tiled=True,
        axis_index_groups=OUT_GROUPS,
    )
    (out,) = call(order_kernel, [((64, 4096), BF16)], [], sent)
    return out


def solution(mesh):
    return jax.shard_map(
        on_device,
        mesh=mesh,
        in_specs=(P(("seq", "head"), None), P("seq", None, "head"), P("head", "seq"), P("head")),
        out_specs=P(("seq", "head"), None),
        check_vma=False,
    )
```
